128 devices in a mesh: seq: 16 (over z_hi, x, core), exp: 8 (over y, z_lo).
Axes of the slice: x: 4, y: 4, z: 4 (z_hi: 2, z_lo: 2; z = z_hi * 2 + z_lo), core: 2. Of those that a mesh axis runs over, the one named last changes fastest.
Arguments:
- tokens: bfloat16 [16384, 2048], P(('seq', 'exp')), may hold values from -6 to 6
- attn_gain: float32 [2048], replicated, may hold values from 0.25 to 1.75
- w_query: bfloat16 [2048, 1536], P(None, 'exp'), may hold values from -0.125 to 0.125
- w_latent: bfloat16 [2048, 576], replicated, may hold values from -0.125 to 0.125
- latent_gain: float32 [512], replicated, may hold values from 0.25 to 1.75
- w_expand: bfloat16 [512, 2048], P(None, 'exp'), may hold values from -0.25 to 0.25
- w_output: bfloat16 [1024, 2048], P('exp'), may hold values from -0.75 to 0.75
- ffn_gain: float32 [2048], replicated, may hold values from 0.25 to 1.75
- route_ids: int32 [16384, 2], P(('seq', 'exp')), may hold values from 0 to 7, all different within a row; in each aligned block of 128 rows (0 to 127, 128 to 255, ...) at most 64 rows name the same one
- route_gates: float32 [16384, 2], P(('seq', 'exp')), may hold values from 0.1 to 1
- w_gate_up: bfloat16 [8, 2048, 2816], P('exp'), may hold values from -0.125 to 0.125
- w_down: bfloat16 [8, 1408, 2048], P('exp'), may hold values from -0.15625 to 0.15625
Outputs:
- layer_out: bfloat16 [16384, 2048], P(('seq', 'exp'))
The draws below stay inside these ranges and needn't reach their ends.
Inputs may be any that keep to these rules, and one draw needn't show every extreme that they name: `route_ids`: each row names 2 different experts; among the rows of one device no expert is named more than 64 times, a bound that some block reaches in some devices' rows.
All inputs are finite; a program needn't handle non-finite values.
Results may differ from the reference program's by a relative error of at most 0.01.
Values may be sent and summed in bfloat16 or wider, within the bound.
No kernel may reach another device: no remote copies, remote signals or barrier semaphores. Data moves between devices by JAX's collectives and lax.ppermute only.
A program may use at most 192 MiB of HBM per device.

```python
import math
import jax
import jax.numpy as jnp
import numpy as np
from jax import lax

D = 2048
FF = 1408
LATENT = 512
ROPE = 64
NOPE = 128
VDIM = 128
H = 8
TOP = 2
TOK_DEV = 128
CAP = 64
EXPERTS = 8
TOKENS = 16384


def levels(key, dims, pieces, smallest, largest):
    level = 1.0
    for dim, parts in pieces:
        steps = jax.random.uniform(jax.random.fold_in(jax.random.fold_in(key, 6), dim), (parts,), jnp.float32, smallest / len(pieces), largest / len(pieces))
        level = level * jnp.repeat(jnp.exp(steps), dims[dim] // parts).reshape((-1,) + (1,) * (len(dims) - 1 - dim))
    return level


def deal_out(key, own, number, rows, amount, top, bound, slope):
    ranking = jax.random.permutation(key, amount)
    heavy_load, ordinary = load_shares(amount, rows * top, bound, slope, True), load_shares(amount, rows * top, bound, slope, False)
    places = jnp.arange(amount)

    def named(lengths, turn):
        used = int((lengths > 0).sum())
        fixed = max(1, used // 4)
        shifted = fixed + (places - fixed + turn * (used - fixed)) % max(1, amount - fixed)
        return jnp.zeros((amount,), jnp.int32).at[ranking[jnp.where(places < fixed, places, shifted)]].set(jnp.asarray(lengths, jnp.int32))

    lengths = jnp.where(number % 4 == 0, named(heavy_load, number // 4), named(ordinary, number - number // 4 - 1))
    mixed = jax.random.permutation(jax.random.fold_in(own, 3), amount)
    source_of, sink = mixed[0:amount // 2 * 2:2], mixed[1:amount // 2 * 2:2]
    slack = jnp.minimum(lengths[source_of] - 1, bound - lengths[sink]) // 2
    slack = jnp.where((source_of == ranking[0]) | (sink == ranking[0]) | (lengths[sink] == 0), 0, jnp.maximum(slack, 0))
    shifted = jax.random.randint(jax.random.fold_in(own, 4), (amount // 2,), 0, 1 << 20) % (slack + 1)
    lengths = lengths.at[source_of].add(-shifted).at[sink].add(shifted)
    labels = jnp.searchsorted(jnp.cumsum(lengths), jnp.arange(rows * top), side="right").astype(jnp.int32)
    table = labels.reshape(top, rows).T
    table = table[jax.random.permutation(jax.random.fold_in(own, 1), rows)]
    turn = jax.random.randint(jax.random.fold_in(own, 2), (rows, 1), 0, top)
    return jnp.take_along_axis(table, (jnp.arange(top)[None, :] + turn) % top, axis=1)


def load_shares(number_of, total, limit, lean, full):
    portions = [(1 << 20) // math.isqrt(standing ** lean) + 1 for standing in range(1, number_of + 1)]
    largest = limit if full else min(limit, max(-(-total // number_of), total * portions[0] // sum(portions)))
    least = 1 if total - largest >= number_of - 1 else 0
    given, surplus = [largest] + [least] * (number_of - 1), total - largest - least * (number_of - 1)
    while surplus > 0:
        free = [i for i in range(1, number_of) if given[i] < largest] or [i for i in range(1, number_of) if given[i] < limit]
        whole, remaining = sum([portions[i] for i in free]), surplus
        for i in free:
            extra = min(limit - given[i], max(1, remaining * portions[i] // whole), surplus)
            given[i] = given[i] + extra
            surplus = surplus - extra
    return np.array(given)


def bell_draw(own_key, shape, scale, bound, cuts=(), kind=jnp.bfloat16):
    entries = scale * jax.random.normal(own_key, shape, jnp.float32)
    if cuts:
        entries = entries * levels(own_key, shape, cuts, -0.22, 0.18)
    return jnp.clip(entries, -bound, bound).astype(kind)


def setup_inputs(seed: int = 0) -> dict:
    key_list = jax.random.split(jax.random.key(seed), 13)
    tokens = bell_draw(key_list[0], (TOKENS, D), 1.0, 6.0, ((0, 128),))
    attn_gain = jnp.clip(1.0 + 0.15 * jax.random.normal(key_list[1], (D,), jnp.float32), 0.25, 1.75)
    w_query = bell_draw(key_list[2], (D, H * (NOPE + ROPE)), D ** -0.5, 0.125, ((1, 8),))
    w_latent = bell_draw(key_list[3], (D, LATENT + ROPE), D ** -0.5, 0.125)
    latent_gain = jnp.clip(1.0 + 0.15 * jax.random.normal(key_list[4], (LATENT,), jnp.float32), 0.25, 1.75)
    w_expand = bell_draw(key_list[5], (LATENT, H * (NOPE + VDIM)), LATENT ** -0.5, 0.25, ((1, 8),))
    w_output = bell_draw(key_list[6], (H * VDIM, D), (H * VDIM // 16) ** -0.5, 0.75, ((0, 8),))
    ffn_gain = jnp.clip(1.0 + 0.15 * jax.random.normal(key_list[7], (D,), jnp.float32), 0.25, 1.75)
    route_ids_keys = jax.random.split(jax.random.fold_in(key_list[8], 1), TOKENS // TOK_DEV)
    route_ids_turns = jax.random.permutation(jax.random.fold_in(key_list[8], 3), TOKENS // TOK_DEV)
    route_ids = jax.vmap(lambda own, number: deal_out(jax.random.fold_in(key_list[8], 2), own, number, TOK_DEV, EXPERTS, TOP, CAP, 2))(route_ids_keys, route_ids_turns).reshape((TOKENS, TOP))
    route_gates = jnp.clip(0.1 + 0.9 * jax.random.uniform(key_list[9], (TOKENS, TOP), jnp.float32) ** levels(key_list[9], (TOKENS, TOP), ((0, 128),), -0.2, 0.2), 0.1, 1.0)
    w_gate_up = bell_draw(key_list[10], (EXPERTS, D, 2 * FF), D ** -0.5, 0.125, ((0, 8),))
    w_down = bell_draw(key_list[11], (EXPERTS, FF, D), FF ** -0.5, 0.15625, ((0, 8),))
    return dict(tokens=tokens, attn_gain=attn_gain, w_query=w_query, w_latent=w_latent, latent_gain=latent_gain, w_expand=w_expand, w_output=w_output, ffn_gain=ffn_gain, route_ids=route_ids, route_gates=route_gates, w_gate_up=w_gate_up, w_down=w_down)


EPS = 1e-06

def scaled(values, gain):
    mean_sq = lax.optimization_barrier(jnp.mean(values * values, axis=-1, keepdims=True))
    return values * lax.rsqrt(mean_sq + EPS) * gain

def angles(positions):
    half = ROPE // 2
    inverse = 10000.0 ** (-(jnp.arange(half, dtype=jnp.float32) * 2.0 / ROPE))
    theta = positions.astype(jnp.float32)[:, None] * inverse[None, :]
    return (jnp.cos(theta), jnp.sin(theta))

def rotate(values, cosine, sine):
    half = ROPE // 2
    first = values[..., :half]
    second = values[..., half:]
    return jnp.concatenate([first * cosine - second * sine, second * cosine + first * sine], axis=-1)

def latents(normed, w_latent, latent_gain, positions):
    mixed_kv = jnp.dot(normed, w_latent, preferred_element_type=jnp.float32)
    latent = scaled(mixed_kv[:, :LATENT], latent_gain).astype(jnp.bfloat16)
    cosine, sine = angles(positions)
    rope_key = rotate(mixed_kv[:, LATENT:], cosine, sine).astype(jnp.bfloat16)
    return (latent, rope_key)

def reference(tokens, attn_gain, w_query, w_latent, latent_gain, w_expand, w_output, ffn_gain, route_ids, route_gates, w_gate_up, w_down):
    total_rows = tokens.shape[0]
    resid = tokens.astype(jnp.float32)
    normed = scaled(resid, attn_gain).astype(jnp.bfloat16)
    positions = jnp.arange(total_rows, dtype=jnp.int32)
    latent, rope_key = latents(normed, w_latent, latent_gain, positions)
    query = jnp.dot(normed, w_query, preferred_element_type=jnp.float32).reshape(total_rows, H, NOPE + ROPE)
    cosine, sine = angles(positions)
    q_nope = jnp.transpose(query[..., :NOPE], (1, 0, 2)).astype(jnp.bfloat16)
    q_rope = jnp.transpose(rotate(query[..., NOPE:], cosine[:, None, :], sine[:, None, :]), (1, 0, 2)).astype(jnp.bfloat16)
    expanded = jnp.dot(latent, w_expand, preferred_element_type=jnp.float32).astype(jnp.bfloat16)
    expanded = jnp.transpose(expanded.reshape(total_rows, H, NOPE + VDIM), (1, 0, 2))
    head_keys = expanded[..., :NOPE]
    head_values = expanded[..., NOPE:]
    scale = (NOPE + ROPE) ** (-0.5)
    q_block = min(total_rows, 1024)

    def head_out(operands):
        query_nope, query_rope, keys, values = operands

        def block_out(index):
            start = (index * q_block).astype(jnp.int32)
            part_nope = lax.dynamic_slice_in_dim(query_nope, start, q_block, 0)
            part_rope = lax.dynamic_slice_in_dim(query_rope, start, q_block, 0)
            scores = jnp.dot(part_nope, keys.T, preferred_element_type=jnp.float32)
            scores = (scores + jnp.dot(part_rope, rope_key.T, preferred_element_type=jnp.float32)) * scale
            q_pos = start + jnp.arange(q_block, dtype=jnp.int32)
            allowed = positions[None, :] <= q_pos[:, None]
            scores = jnp.where(allowed, scores, jnp.float32(0.0))
            weights = jnp.where(allowed, jnp.exp(scores), jnp.float32(0.0))
            total = lax.optimization_barrier(jnp.sum(weights, axis=-1, keepdims=True))
            summed = jnp.dot(weights.astype(jnp.bfloat16), values, preferred_element_type=jnp.float32)
            return (summed / total).astype(jnp.bfloat16)
        blocks = lax.map(block_out, jnp.arange(total_rows // q_block, dtype=jnp.int32))
        return blocks.reshape(total_rows, VDIM)
    attended = lax.map(head_out, (q_nope, q_rope, head_keys, head_values))
    out_w = w_output.reshape(H, VDIM, w_output.shape[1]).astype(jnp.float32)
    attn_out = jnp.einsum('hqd,hdn->qn', attended.astype(jnp.float32), out_w)
    mixed = resid + attn_out
    normed2 = scaled(mixed, ffn_gain).astype(jnp.bfloat16)

    def expert_step(acc, index):
        gate_up = jnp.dot(normed2, w_gate_up[index], preferred_element_type=jnp.float32)
        hidden = (jax.nn.silu(gate_up[:, :FF]) * gate_up[:, FF:]).astype(jnp.bfloat16)
        result = jnp.dot(hidden, w_down[index], preferred_element_type=jnp.float32).astype(jnp.bfloat16)
        weight = lax.optimization_barrier(jnp.sum(jnp.where(route_ids == index, route_gates, jnp.float32(0.0)), axis=1))
        return (acc + weight[:, None] * result.astype(jnp.float32), None)
    moe, unused = lax.scan(expert_step, jnp.zeros(mixed.shape, jnp.float32), jnp.arange(EXPERTS, dtype=jnp.int32))
    return (mixed + moe).astype(jnp.bfloat16)
```

```python
import functools

import jax
import jax.numpy as jnp
from jax import lax
from jax.experimental import pallas as pl
from jax.experimental.pallas import tpu as pltpu
from jax.sharding import PartitionSpec as P

FF = 1408
LATENT = 512
ROPE = 64
NOPE = 128
VDIM = 128
CAP = 64

EPS = 1e-06
QTILE = 256
LOG2E = 1.4426950408889634
SCALE2 = (NOPE + ROPE) ** (-0.5) * LOG2E

XS, YS = 4, 4


def seq_perm(move):
    return [
        (z * 8 + x * 2 + c, move(z, x, c))
        for z in range(2) for x in range(XS) for c in range(2)
    ]


def shift_x(step):
    return seq_perm(lambda z, x, c: z * 8 + ((x + step) % XS) * 2 + c)


SIBLING = seq_perm(lambda z, x, c: z * 8 + x * 2 + 1 - c)
Z_DOWN = [(8 + t, t) for t in range(8)]
Z_UP = [(t, 8 + t) for t in range(8)]
Z_LO = [(e, e ^ 1) for e in range(8)]


def shift_y(step):
    return [(y * 2 + z, ((y + step) % YS) * 2 + z) for y in range(YS) for z in range(2)]


def scaled(values, gain):
    mean_sq = jnp.mean(values * values, axis=-1, keepdims=True)
    return values * lax.rsqrt(mean_sq + EPS) * gain


def angles(positions):
    half = ROPE // 2
    inverse = 10000.0 ** (-(jnp.arange(half, dtype=jnp.float32) * 2.0 / ROPE))
    theta = positions.astype(jnp.float32)[:, None] * inverse[None, :]
    return (jnp.cos(theta), jnp.sin(theta))


def rotate(values, cosine, sine):
    half = ROPE // 2
    first = values[..., :half]
    second = values[..., half:]
    return jnp.concatenate(
        [first * cosine - second * sine, second * cosine + first * sine], axis=-1
    )


def attend_kernel(count, has_carry, modes, qa, qb, *refs):
    packs = refs[:count]
    refs = refs[count:]
    if has_carry:
        o_in, l_in, o_out, l_out = refs
        o_out[...] = o_in[...]
        l_out[...] = l_in[...]
    else:
        o_out, l_out = refs
        o_out[...] = jnp.zeros_like(o_out)
        l_out[...] = jnp.zeros_like(l_out)
    rows = qa.shape[0]
    half = rows // 2
    turn = modes[count]

    def tile(pack, at, diag):
        here = pl.ds(pl.multiple_of(at * QTILE, QTILE), QTILE)
        out = jnp.zeros((QTILE, VDIM), jnp.float32)
        total = jnp.zeros((QTILE, 128), jnp.float32)
        for part in range(2):
            span = slice(part * half, (part + 1) * half)
            keys = jnp.concatenate([pack[span, :], pack[2 * rows:2 * rows + half, :]], axis=1)
            values = pack[rows + part * half:rows + (part + 1) * half, :]
            query = (qa if part == 0 else qb)[here, :]
            scores = lax.dot_general(
                query, keys, (((1,), (1,)), ((), ())), preferred_element_type=jnp.float32
            )
            weights = jnp.exp2(scores * SCALE2)
            if diag:
                q_pos = lax.broadcasted_iota(jnp.int32, (QTILE, half), 0) + at * QTILE
                k_pos = lax.broadcasted_iota(jnp.int32, (QTILE, half), 1) + part * half
                q_pos = (q_pos + turn) & (rows - 1)
                k_pos = (k_pos + turn) & (rows - 1)
                weights = jnp.where(k_pos <= q_pos, weights, 0.0)
            for lane in range(half // 128):
                total = total + weights[:, lane * 128:(lane + 1) * 128]
            out = out + jnp.dot(
                weights.astype(jnp.bfloat16), values, preferred_element_type=jnp.float32
            )
        o_out[here, :] += out
        l_out[here, :] += total

    for i in range(count):
        for mode in (1, 2):
            @pl.when(modes[i] == mode)
            def _():
                def step(at, _):
                    tile(packs[i], at, mode == 2)
                    return 0
                lax.fori_loop(0, rows // QTILE, step, 0)


def attend(modes, qa, qb, packs, carry=None):
    count = len(packs)
    rows = qa.shape[0]
    out = (
        jax.ShapeDtypeStruct((rows, VDIM), jnp.float32),
        jax.ShapeDtypeStruct((rows, 128), jnp.float32),
    )
    vmem = pl.BlockSpec(memory_space=pltpu.VMEM)
    extra = [] if carry is None else list(carry)
    return pl.pallas_call(
        functools.partial(attend_kernel, count, carry is not None),
        out_shape=out,
        in_specs=[pl.BlockSpec(memory_space=pltpu.SMEM)] + [vmem] * (2 + count + len(extra)),
        out_specs=(vmem, vmem),
        compiler_params=pltpu.CompilerParams(vmem_limit_bytes=40 * 1024 * 1024),
        cost_estimate=pl.CostEstimate(
            flops=count * rows * rows * 640, bytes_accessed=count * rows * 640, transcendentals=count * rows * rows
        ),
    )(modes, qa, qb, *packs, *extra)


def body(
    tokens,
    attn_gain,
    w_query,
    w_latent,
    latent_gain,
    w_expand,
    w_output,
    ffn_gain,
    route_ids,
    route_gates,
    w_gate_up,
    w_down,
):
    rows = tokens.shape[0]
    groups = lax.axis_size("exp")
    span = rows * groups
    seq_at = lax.axis_index("seq")
    exp_at = lax.axis_index("exp")
    z_hi, x_at, core = seq_at // 8, (seq_at // 2) % XS, seq_at % 2
    y_at, z_lo = exp_at // 2, exp_at % 2
    block_first = seq_at * span

    half_d = tokens.shape[1] // 2
    wq_t = jnp.transpose(w_query)
    wq_half = lax.dynamic_slice_in_dim(wq_t, core * half_d, half_d, 1)
    wq_mine = [lax.ppermute(wq_half, "exp", shift_y(-j)) for j in (1, 2, 3)]
    wq_mine = jnp.concatenate(wq_mine, axis=0)
    wq_other = lax.ppermute(wq_mine, "seq", SIBLING)

    partner = lax.ppermute(tokens, "exp", Z_LO)
    pair = jnp.where(
        z_lo == 0,
        jnp.concatenate([tokens, partner], axis=0),
        jnp.concatenate([partner, tokens], axis=0),
    )
    normed = scaled(pair.astype(jnp.float32), attn_gain).astype(jnp.bfloat16)
    pos = block_first + y_at * (2 * rows) + jnp.arange(2 * rows, dtype=jnp.int32)
    cosine, sine = angles(pos)

    mixed_kv = jnp.dot(normed, w_latent, preferred_element_type=jnp.float32)
    latent = scaled(mixed_kv[:, :LATENT], latent_gain).astype(jnp.bfloat16)
    rope_key = rotate(mixed_kv[:, LATENT:], cosine, sine).astype(jnp.bfloat16)
    piece = jnp.concatenate([latent, rope_key], axis=1)
    pieces = [piece] + [lax.ppermute(piece, "exp", shift_y(-j)) for j in (1, 2, 3)]
    pieces = jnp.concatenate(pieces, axis=0)
    expanded = jnp.dot(
        pieces[:, :LATENT], w_expand, preferred_element_type=jnp.float32
    ).astype(jnp.bfloat16)
    ropes = pieces[:, LATENT:]
    pack = jnp.concatenate(
        [
            expanded[:, :NOPE],
            expanded[:, NOPE:],
            jnp.concatenate([ropes[:span // 2], ropes[span // 2:]], axis=1),
        ],
        axis=0,
    )

    flipped = jnp.where(
        core == 0,
        normed,
        jnp.concatenate([normed[:, half_d:], normed[:, :half_d]], axis=1),
    )
    own_q = jnp.dot(normed, w_query, preferred_element_type=jnp.float32)
    other_q = lax.dot_general(
        flipped,
        jnp.concatenate([wq_mine, wq_other], axis=1),
        (((1,), (1,)), ((), ())),
        preferred_element_type=jnp.float32,
    )
    q_parts = []
    width = NOPE + ROPE
    for j in range(YS):
        part = own_q if j == 0 else other_q[:, (j - 1) * width:j * width]
        part = jnp.concatenate(
            [part[:, :NOPE], rotate(part[:, NOPE:], cosine, sine)], axis=1
        ).astype(jnp.bfloat16)
        q_parts.append(part)
    queries = [q_parts[0]] + [
        lax.ppermute(q_parts[(YS - j) % YS], "exp", shift_y(-j)) for j in (1, 2, 3)
    ]
    queries = jnp.concatenate(queries, axis=0)
    q_nope, q_rope = queries[:, :NOPE], queries[:, NOPE:]
    q_pack = jnp.concatenate(
        [q_nope, jnp.concatenate([q_rope[:span // 2], q_rope[span // 2:]], axis=1)], axis=0
    )
    far_pack = lax.ppermute(q_pack, "seq", Z_DOWN)

    def spread(packed):
        nope, ropes = packed[:span], packed[span:]
        ropes = jnp.concatenate([ropes[:, :ROPE], ropes[:, ROPE:]], axis=0)
        blank = jnp.zeros_like(ropes)
        return (
            jnp.concatenate([nope, ropes, blank], axis=1),
            jnp.concatenate([nope, blank, ropes], axis=1),
        )

    first_q = spread(jnp.where(z_hi == 0, far_pack, q_pack))
    second_q = spread(q_pack)

    gathered = [pack] + [lax.ppermute(pack, "seq", shift_x(-j)) for j in (1, 3, 2)]
    packs, at_plane = [], []
    for j, held in zip((0, 1, 3, 2), gathered):
        packs += [held, lax.ppermute(held, "seq", SIBLING)]
        base = ((x_at + j) % XS) * 2
        at_plane += [base + core, base + 1 - core]
    here = x_at * 2 + core
    at_plane = jnp.stack(at_plane)
    causal = jnp.where(at_plane < here, 1, jnp.where(at_plane == here, 2, 0))
    turn = jnp.reshape(y_at * (2 * rows), (1,))
    first_modes = jnp.where(z_hi == 0, 1, causal)
    second_modes = jnp.where(z_hi == 0, causal, 0)
    carry = None
    for at in range(0, 8, 2):
        modes = jnp.concatenate([first_modes[at:at + 2], turn]).astype(jnp.int32)
        carry = attend(modes, *first_q, packs[at:at + 2], carry)
    first_o, first_l = carry
    first = jnp.concatenate([first_o, jnp.sum(first_l, axis=1).reshape(span // 128, 128)], axis=0)
    arrived = lax.ppermute(first, "seq", Z_UP)
    second_o, second_l = attend(
        jnp.concatenate([second_modes, turn]).astype(jnp.int32), *second_q, packs
    )
    kept = jnp.where(z_hi == 0, 0.0, 1.0)
    summed = second_o + kept * (first_o + arrived[:span])
    total = jnp.sum(second_l, axis=1) + kept * (
        jnp.sum(first_l, axis=1) + arrived[span:].reshape(span)
    )
    attended = (summed / total[:, None]).astype(jnp.bfloat16)

    twice = jnp.concatenate([attended, attended], axis=0)
    attended = lax.dynamic_slice_in_dim(
        twice, jnp.where(y_at == 0, 0, span - y_at * (2 * rows)), span, 0
    )
    by_head = lax.all_to_all(
        attended.reshape(groups, rows, VDIM), "exp", split_axis=0, concat_axis=0, tiled=True
    )
    by_head = jnp.transpose(by_head, (1, 0, 2)).reshape(rows, groups * VDIM)

    half_o = w_output.shape[0] // 2
    wo_half = lax.dynamic_slice_in_dim(w_output, core * half_o, half_o, 0)
    whole_o = jnp.zeros((groups, 2, half_o, w_output.shape[1]), jnp.bfloat16)
    fetched = [wo_half] + [
        lax.ppermute(wo_half, "exp", [((e ^ j), e) for e in range(8)]) for j in range(1, 8)
    ]
    fetched = jnp.stack(fetched)
    fetched_other = lax.ppermute(fetched, "seq", SIBLING)
    order = jnp.bitwise_xor(exp_at, jnp.arange(groups, dtype=jnp.int32))
    heads_in = by_head.reshape(rows, groups, 2, half_o)
    heads_in = jnp.take(heads_in, order, axis=1)
    mine = jnp.where(core == 0, heads_in[:, :, 0], heads_in[:, :, 1]).reshape(rows, -1)
    others = jnp.where(core == 0, heads_in[:, :, 1], heads_in[:, :, 0]).reshape(rows, -1)
    model_width = w_output.shape[1]
    projected = jnp.dot(
        mine, fetched.reshape(-1, model_width), preferred_element_type=jnp.float32
    ) + jnp.dot(
        others, fetched_other.reshape(-1, model_width), preferred_element_type=jnp.float32
    )
    mixed = tokens.astype(jnp.float32) + projected
    normed2 = scaled(mixed, ffn_gain).astype(jnp.bfloat16)

    local_experts = w_gate_up.shape[0]
    experts = local_experts * groups
    expert_ids = jnp.arange(experts, dtype=jnp.int32)
    picked = route_ids[:, :, None] == expert_ids[None, None, :]
    picks = jnp.sum(picked.astype(jnp.int32), axis=1)
    weight = jnp.sum(jnp.where(picked, route_gates[:, :, None], 0.0), axis=1)
    slot = jnp.cumsum(picks, axis=0) - picks
    placed = (slot[:, :, None] == jnp.arange(CAP, dtype=jnp.int32)[None, None, :]) & (
        picks[:, :, None] > 0
    )
    dispatch = placed.astype(jnp.bfloat16)
    outgoing = jnp.einsum(
        "tec,td->ecd", dispatch, normed2, preferred_element_type=jnp.float32
    ).astype(jnp.bfloat16)
    width = normed2.shape[1]
    arrived_rows = lax.all_to_all(outgoing, "exp", split_axis=0, concat_axis=0, tiled=True)
    sources = arrived_rows.shape[0] // local_experts
    items = arrived_rows.shape[1]
    grouped = arrived_rows.reshape(sources, local_experts, items, width)
    gate_up = jnp.einsum("sltd,ldf->sltf", grouped, w_gate_up, preferred_element_type=jnp.float32)
    hidden = (jax.nn.silu(gate_up[..., :FF]) * gate_up[..., FF:]).astype(jnp.bfloat16)
    result = jnp.einsum(
        "sltf,lfd->sltd", hidden, w_down, preferred_element_type=jnp.float32
    ).astype(jnp.bfloat16)
    result = result.reshape(sources * local_experts, items, width)
    returned = lax.all_to_all(result, "exp", split_axis=0, concat_axis=0, tiled=True)
    combine = placed.astype(jnp.float32) * weight[:, :, None]
    moe = jnp.einsum(
        "tec,ecd->td", combine, returned.astype(jnp.float32), precision=lax.Precision.HIGHEST
    )
    return (mixed + moe).astype(jnp.bfloat16)


def solution(mesh):
    placed = (
        P(("seq", "exp"), None),
        P(),
        P(None, "exp"),
        P(),
        P(),
        P(None, "exp"),
        P("exp", None),
        P(),
        P(("seq", "exp"), None),
        P(("seq", "exp"), None),
        P("exp", None, None),
        P("exp", None, None),
    )
    return jax.shard_map(
        body, mesh=mesh, in_specs=placed, out_specs=P(("seq", "exp"), None), check_vma=False
    )
```

```python
import functools

import jax
import jax.numpy as jnp
from jax import lax
from jax.experimental import pallas as pl
from jax.experimental.pallas import tpu as pltpu
from jax.sharding import PartitionSpec as P

FF = 1408
LATENT = 512
ROPE = 64
NOPE = 128
VDIM = 128
CAP = 64

EPS = 1e-06
UNIT = 1280
ROWS_BY_ROWS = (((1,), (1,)), ((), ()))
LOG2E = 1.4426950408889634
SCALE2 = (NOPE + ROPE) ** (-0.5) * LOG2E

XS, YS = 4, 4


def seq_perm(move):
    return [
        (z * 8 + x * 2 + c, move(z, x, c))
        for z in range(2) for x in range(XS) for c in range(2)
    ]


def shift_x(step):
    return seq_perm(lambda z, x, c: z * 8 + ((x + step) % XS) * 2 + c)


SIBLING = seq_perm(lambda z, x, c: z * 8 + x * 2 + 1 - c)
Z_DOWN = [(8 + t, t) for t in range(8)]
Z_UP = [(t, 8 + t) for t in range(8)]
Z_LO = [(e, e ^ 1) for e in range(8)]


def shift_y(step):
    return [(y * 2 + z, ((y + step) % YS) * 2 + z) for y in range(YS) for z in range(2)]


def scaled(values, gain):
    mean_sq = jnp.mean(values * values, axis=-1, keepdims=True)
    return values * lax.rsqrt(mean_sq + EPS) * gain


def angles(positions):
    half = ROPE // 2
    inverse = 10000.0 ** (-(jnp.arange(half, dtype=jnp.float32) * 2.0 / ROPE))
    theta = positions.astype(jnp.float32)[:, None] * inverse[None, :]
    return (jnp.cos(theta), jnp.sin(theta))


def rotate(values, cosine, sine):
    half = ROPE // 2
    first = values[..., :half]
    second = values[..., half:]
    return jnp.concatenate(
        [first * cosine - second * sine, second * cosine + first * sine], axis=-1
    )


def latent_kernel(tokens, gain, w_latent, latent_gain, cosine, sine, normed_out, piece_out):
    resid = tokens[...].astype(jnp.float32)
    normed = scaled(resid, gain[...]).astype(jnp.bfloat16)
    normed_out[...] = normed
    mixed_kv = lax.dot_general(
        normed, w_latent[...], ROWS_BY_ROWS, preferred_element_type=jnp.float32
    )
    piece_out[:, :LATENT] = scaled(mixed_kv[:, :LATENT], latent_gain[...]).astype(jnp.bfloat16)
    piece_out[:, LATENT:] = rotate(mixed_kv[:, LATENT:], cosine[...], sine[...]).astype(jnp.bfloat16)


def own_latents(tokens, gain, w_latent, latent_gain, cosine, sine):
    rows, width = tokens.shape
    vmem = pl.BlockSpec(memory_space=pltpu.VMEM)
    return pl.pallas_call(
        latent_kernel,
        out_shape=(
            jax.ShapeDtypeStruct((rows, width), jnp.bfloat16),
            jax.ShapeDtypeStruct((rows, LATENT + ROPE), jnp.bfloat16),
        ),
        in_specs=[vmem] * 6,
        out_specs=(vmem, vmem),
        compiler_params=pltpu.CompilerParams(vmem_limit_bytes=24 * 1024 * 1024),
        cost_estimate=pl.CostEstimate(
            flops=2 * rows * width * (LATENT + ROPE),
            bytes_accessed=2 * width * (LATENT + ROPE),
            transcendentals=0,
        ),
    )(tokens, gain[None], jnp.transpose(w_latent), latent_gain[None], cosine, sine)


def pack_kernel(p0, p1, p2, p3, w_expand, out):
    for at, piece in enumerate((p0, p1, p2, p3)):
        base, part = (at // 2) * UNIT, at % 2
        rows = piece.shape[0]
        expanded = jnp.dot(
            piece[:, :LATENT], w_expand[...], preferred_element_type=jnp.float32
        ).astype(jnp.bfloat16)
        out[base + part * rows:base + (part + 1) * rows, :] = expanded[:, :NOPE]
        out[base + (2 + part) * rows:base + (3 + part) * rows, :] = expanded[:, NOPE:]
        out[base + 4 * rows:base + 5 * rows, part * ROPE:(part + 1) * ROPE] = piece[:, LATENT:]


def make_pack(pieces, w_expand):
    vmem = pl.BlockSpec(memory_space=pltpu.VMEM)
    return pl.pallas_call(
        pack_kernel,
        out_shape=jax.ShapeDtypeStruct((2 * UNIT, 128), jnp.bfloat16),
        in_specs=[vmem] * 5,
        out_specs=vmem,
        compiler_params=pltpu.CompilerParams(vmem_limit_bytes=16 * 1024 * 1024),
        cost_estimate=pl.CostEstimate(
            flops=2 * 1024 * LATENT * 256, bytes_accessed=2 * 1024 * 1024, transcendentals=0
        ),
    )(*pieces, w_expand)


def query_kernel(place, own, partner, w_own, *refs):
    weights, refs = refs[:8], refs[8:]
    cosine, sine = refs[:2]
    outs, held = refs[2:6], refs[6]
    rows, width = own.shape
    held[:rows, :] = own[...]
    held[rows:, :] = partner[...]
    chunk = width // 8
    others = 0.0
    for i, weight in enumerate(weights):
        at = ((place[0] + i % XS) % XS) * 2 + (place[1] + i // XS) % 2
        others = others + lax.dot_general(
            held[:, pl.ds(pl.multiple_of(at * chunk, chunk), chunk)], weight[...],
            ROWS_BY_ROWS, preferred_element_type=jnp.float32,
        )
    size = NOPE + ROPE
    for j, out in enumerate(outs):
        if j == 0:
            query = lax.dot_general(
                held[...], w_own[...], ROWS_BY_ROWS, preferred_element_type=jnp.float32
            )
        else:
            query = others[:, (j - 1) * size:j * size]
        out[:2 * rows, :] = query[:, :NOPE].astype(jnp.bfloat16)
        ropes = rotate(query[:, NOPE:], cosine[...], sine[...]).astype(jnp.bfloat16)
        out[2 * rows:, :ROPE] = ropes[:rows]
        out[2 * rows:, ROPE:] = ropes[rows:]


def make_queries(place, own, partner, w_own, chunks, cosine, sine):
    rows, width = own.shape
    vmem = pl.BlockSpec(memory_space=pltpu.VMEM)
    return pl.pallas_call(
        query_kernel,
        out_shape=(jax.ShapeDtypeStruct((3 * rows, 128), jnp.bfloat16),) * YS,
        in_specs=[pl.BlockSpec(memory_space=pltpu.SMEM)] + [vmem] * 13,
        out_specs=(vmem,) * YS,
        scratch_shapes=[pltpu.VMEM((2 * rows, width), jnp.bfloat16)],
        compiler_params=pltpu.CompilerParams(vmem_limit_bytes=16 * 1024 * 1024),
        cost_estimate=pl.CostEstimate(
            flops=4 * rows * width * 768, bytes_accessed=2 * width * 768, transcendentals=0
        ),
    )(place, own, partner, w_own, *chunks, cosine, sine)


def attend_kernel(sizes, far, has_carry, last, modes, *refs):
    count = len(sizes)
    q_refs, refs = refs[:1 + far], refs[1 + far:]
    packs = refs[:count]
    refs, (qa, qb) = refs[count:-2], refs[-2:]
    o_out, l_out = refs[-2:]
    rows = qa.shape[0]
    packed, o_out = o_out, o_out.at[pl.ds(0, rows), :]
    if has_carry:
        o_out[...] = refs[0][...]
        l_out[...] = refs[1][...]
    else:
        o_out[...] = jnp.zeros_like(o_out)
        l_out[...] = jnp.zeros_like(l_out)
    part_rows = UNIT // 5

    def spread(source):
        some = part_rows // 2
        left = lax.broadcasted_iota(jnp.int32, (some, 128), 1) < ROPE
        blank = jnp.zeros((some, 128), jnp.bfloat16)
        for piece in range(rows // part_rows):
            base = piece * 3 * some
            ropes = source[base + part_rows:base + 3 * some, :]
            turned = jnp.concatenate([ropes[:, ROPE:], ropes[:, :ROPE]], axis=1)
            for side in range(2):
                here = slice(piece * part_rows + side * some, piece * part_rows + (side + 1) * some)
                nope = source[base + side * some:base + (side + 1) * some, :]
                qa[here, :NOPE] = nope
                qb[here, :NOPE] = nope
                qa[here, NOPE:] = jnp.where(left, ropes if side == 0 else turned, blank)
                qb[here, NOPE:] = jnp.where(left, blank, turned if side == 0 else ropes)

    if far:
        pl.when(modes[count + 2] == 0)(functools.partial(spread, q_refs[0]))
        pl.when(modes[count + 2] == 1)(functools.partial(spread, q_refs[1]))
    else:
        spread(q_refs[0])

    def position(index):
        return ((index + modes[count] * part_rows) & (rows - 1)) ^ (modes[count + 1] * 128)

    def visit(pack, diag):
        out = o_out[...]
        total = l_out[...]
        for unit in range(pack.shape[0] // UNIT):
            base = unit * UNIT
            for part in range(2):
                keys = jnp.concatenate(
                    [
                        pack[base + part * part_rows:base + (part + 1) * part_rows, :],
                        pack[base + 4 * part_rows:base + 5 * part_rows, :],
                    ],
                    axis=1,
                )
                values = pack[base + (2 + part) * part_rows:base + (3 + part) * part_rows, :]
                query = (qa if part == 0 else qb)[...]
                scores = lax.dot_general(
                    query, keys, ROWS_BY_ROWS, preferred_element_type=jnp.float32
                )
                weights = jnp.exp2(scores * SCALE2)
                if diag:
                    q_pos = position(lax.broadcasted_iota(jnp.int32, weights.shape, 0))
                    k_pos = position(
                        lax.broadcasted_iota(jnp.int32, weights.shape, 1)
                        + (unit * 2 + part) * part_rows
                    )
                    weights = jnp.where(k_pos <= q_pos, weights, 0.0)
                for lane in range(part_rows // 128):
                    total = total + weights[:, lane * 128:(lane + 1) * 128]
                out = out + jnp.dot(
                    weights.astype(jnp.bfloat16), values, preferred_element_type=jnp.float32
                )
        o_out[...] = out
        l_out[...] = total

    for i in range(count):
        pl.when(modes[i] == 1)(functools.partial(visit, packs[i], False))
    if not has_carry:
        pl.when(modes[0] == 2)(functools.partial(visit, packs[0], True))
    if last:
        lanes = lax.broadcasted_iota(jnp.int32, (128, 128), 1)
        sums = jnp.zeros((128, 128), jnp.float32)
        for group in range(rows // 128):
            total = jnp.sum(l_out[group * 128:(group + 1) * 128, :], axis=1, keepdims=True)
            sums = jnp.where(lanes == group, total, sums)
        packed[pl.ds(rows, 128), :] = sums


def attend(modes, queries, packs, carry=None, last=False):
    rows = 1024
    vmem = pl.BlockSpec(memory_space=pltpu.VMEM)
    sums = jax.ShapeDtypeStruct((rows, 128), jnp.float32)
    scratch = [pltpu.VMEM((rows, 256), jnp.bfloat16)] * 2
    if last:
        out = jax.ShapeDtypeStruct((rows + 128, VDIM), jnp.float32)
        out_specs, scratch = vmem, [pltpu.VMEM((rows, 128), jnp.float32)] + scratch
    else:
        out, out_specs = (sums, sums), (vmem, vmem)
    extra = [] if carry is None else list(carry)
    sizes = tuple(p.shape[0] for p in packs)
    keys = sum(sizes) // UNIT * 512
    operands = [*queries, *packs, *extra]
    return pl.pallas_call(
        functools.partial(attend_kernel, sizes, len(queries) - 1, carry is not None, last),
        out_shape=out,
        in_specs=[pl.BlockSpec(memory_space=pltpu.SMEM)] + [vmem] * len(operands),
        out_specs=out_specs,
        scratch_shapes=scratch,
        compiler_params=pltpu.CompilerParams(vmem_limit_bytes=24 * 1024 * 1024),
        cost_estimate=pl.CostEstimate(
            flops=rows * keys * 768, bytes_accessed=keys * 640, transcendentals=rows * keys
        ),
    )(modes, *operands)


def finish_kernel(flags, first, far, second, out):
    rows = 128
    count = out.shape[0] // rows
    kept = flags[0].astype(jnp.float32)
    lanes = lax.broadcasted_iota(jnp.int32, (rows, 128), 1)
    tail = pl.ds(count * rows, rows)
    totals = second[tail, :] + kept * (first[tail, :] + far[tail, :])
    for chunk in range(count):
        span = slice(chunk * rows, (chunk + 1) * rows)
        summed = second[span, :] + kept * (first[span, :] + far[span, :])
        total = jnp.sum(jnp.where(lanes == chunk, totals, 0.0), axis=1, keepdims=True)
        at = (((flags[1] + chunk // 2) & 3) * 2 + ((chunk % 2) ^ flags[2])) * rows
        out[pl.ds(pl.multiple_of(at, rows), rows), :] = (summed / total).astype(jnp.bfloat16)


def finish(flags, first, far, second):
    vmem = pl.BlockSpec(memory_space=pltpu.VMEM)
    return pl.pallas_call(
        finish_kernel,
        out_shape=jax.ShapeDtypeStruct((first.shape[0] - 128, VDIM), jnp.bfloat16),
        in_specs=[pl.BlockSpec(memory_space=pltpu.SMEM)] + [vmem] * 3,
        out_specs=vmem,
        compiler_params=pltpu.CompilerParams(vmem_limit_bytes=16 * 1024 * 1024),
    )(flags, first, far, second)


def middle_kernel(flags, by_head, *refs):
    shares, refs = refs[:8], refs[8:]
    tokens, gain, chosen = refs[:3]
    mixed, out, held = refs[3:]
    rows, half = tokens.shape[0], shares[0].shape[1]
    for l in range(8):
        held[:, l * VDIM:(l + 1) * VDIM] = by_head[flags[1 + l]]
    for side in range(2):
        at = pl.multiple_of(jnp.where(flags[0] == side, 0, half), half)
        total = tokens[:, pl.ds(at, half)].astype(jnp.float32)
        for j in range(YS):
            total = total + jnp.dot(
                held[:, j * 256:(j + 1) * 256], shares[side * 4 + j][...],
                preferred_element_type=jnp.float32,
            )
        mixed[:, pl.ds(at, half)] = total
    normed = scaled(mixed[...], gain[...]).astype(jnp.bfloat16)
    for e in range(out.shape[0]):
        out[e] = jnp.dot(
            chosen[e * CAP:(e + 1) * CAP, :], normed, preferred_element_type=jnp.float32
        ).astype(jnp.bfloat16)


def middle(flags, by_head, shares, tokens, gain, chosen):
    rows, width = tokens.shape
    vmem = pl.BlockSpec(memory_space=pltpu.VMEM)
    return pl.pallas_call(
        middle_kernel,
        out_shape=(
            jax.ShapeDtypeStruct((rows, width), jnp.float32),
            jax.ShapeDtypeStruct((8, CAP, width), jnp.bfloat16),
        ),
        in_specs=[pl.BlockSpec(memory_space=pltpu.SMEM)] + [vmem] * 12,
        out_specs=(vmem,) * 2,
        scratch_shapes=[pltpu.VMEM((rows, 8 * VDIM), jnp.bfloat16)],
        compiler_params=pltpu.CompilerParams(vmem_limit_bytes=20 * 1024 * 1024),
        cost_estimate=pl.CostEstimate(
            flops=4 * rows * width * 1024, bytes_accessed=8 * width * 1024, transcendentals=0
        ),
    )(flags, by_head, *shares, tokens, gain[None], chosen)


FF_STEPS = FF // 128
DOWN_STEPS = 8


def expert_kernel(arrived, w_gate_up, w_down, out, gate_up, down, hidden, gate_sem, up_sem, down_sem):
    experts, items, width = arrived.shape
    cols = width // DOWN_STEPS

    def gate_copies(i):
        at = pl.ds(pl.multiple_of(i * 128, 128), 128)
        up = pl.ds(pl.multiple_of(FF + i * 128, 128), 128)
        return (
            pltpu.make_async_copy(w_gate_up.at[0, :, at], gate_up.at[:, at], gate_sem.at[i]),
            pltpu.make_async_copy(w_gate_up.at[0, :, up], gate_up.at[:, up], up_sem.at[i]),
        )

    def down_copy(i):
        at = pl.ds(pl.multiple_of(i * cols, cols), cols)
        return pltpu.make_async_copy(w_down.at[0, :, at], down.at[:, at], down_sem.at[i])

    for i in range(FF_STEPS):
        for copy in gate_copies(i):
            copy.start()
    for i in range(DOWN_STEPS):
        down_copy(i).start()
    rows = arrived[...].reshape(experts * items, width)

    def first(i, _):
        for copy in gate_copies(i):
            copy.wait()
        at = pl.ds(pl.multiple_of(i * 128, 128), 128)
        up = pl.ds(pl.multiple_of(FF + i * 128, 128), 128)
        both = jnp.concatenate([gate_up[:, at], gate_up[:, up]], axis=1)
        product = jnp.dot(rows, both, preferred_element_type=jnp.float32)
        hidden[:, at] = (jax.nn.silu(product[:, :128]) * product[:, 128:]).astype(jnp.bfloat16)
        return 0

    def second(i, _):
        down_copy(i).wait()
        at = pl.ds(pl.multiple_of(i * cols, cols), cols)
        result = jnp.dot(hidden[...], down[:, at], preferred_element_type=jnp.float32)
        out[:, :, at] = result.astype(jnp.bfloat16).reshape(experts, items, cols)
        return 0

    lax.fori_loop(0, FF_STEPS, first, 0)
    lax.fori_loop(0, DOWN_STEPS, second, 0)


def expert(arrived, w_gate_up, w_down):
    experts, items, width = arrived.shape
    vmem = pl.BlockSpec(memory_space=pltpu.VMEM)
    return pl.pallas_call(
        expert_kernel,
        out_shape=jax.ShapeDtypeStruct(arrived.shape, jnp.bfloat16),
        in_specs=[vmem, pl.BlockSpec(memory_space=pl.ANY), pl.BlockSpec(memory_space=pl.ANY)],
        out_specs=vmem,
        scratch_shapes=[
            pltpu.VMEM((width, 2 * FF), jnp.bfloat16),
            pltpu.VMEM((FF, width), jnp.bfloat16),
            pltpu.VMEM((experts * items, FF), jnp.bfloat16),
            pltpu.SemaphoreType.DMA((FF_STEPS,)),
            pltpu.SemaphoreType.DMA((FF_STEPS,)),
            pltpu.SemaphoreType.DMA((DOWN_STEPS,)),
        ],
        compiler_params=pltpu.CompilerParams(vmem_limit_bytes=48 * 1024 * 1024),
        cost_estimate=pl.CostEstimate(
            flops=6 * experts * items * width * FF, bytes_accessed=6 * width * FF, transcendentals=0
        ),
    )(arrived, w_gate_up, w_down)


def combine_kernel(mixed, gates, returned, out):
    rows = mixed.shape[0]
    first = gates[...].astype(jnp.bfloat16)
    rest = gates[...] - first.astype(jnp.float32)
    second = rest.astype(jnp.bfloat16)
    third = (rest - second.astype(jnp.float32)).astype(jnp.bfloat16)
    stacked = jnp.concatenate([first, second, third], axis=0)
    moe = jnp.dot(
        stacked, returned[...].reshape(gates.shape[1], mixed.shape[1]),
        preferred_element_type=jnp.float32,
    )
    moe = moe[:rows] + (moe[rows:2 * rows] + moe[2 * rows:])
    out[...] = (mixed[...] + moe).astype(jnp.bfloat16)


def combine(mixed, gates, returned):
    vmem = pl.BlockSpec(memory_space=pltpu.VMEM)
    return pl.pallas_call(
        combine_kernel,
        out_shape=jax.ShapeDtypeStruct(mixed.shape, jnp.bfloat16),
        in_specs=[vmem] * 3,
        out_specs=vmem,
        compiler_params=pltpu.CompilerParams(vmem_limit_bytes=24 * 1024 * 1024),
    )(mixed, gates, returned)


def body(
    tokens,
    attn_gain,
    w_query,
    w_latent,
    latent_gain,
    w_expand,
    w_output,
    ffn_gain,
    route_ids,
    route_gates,
    w_gate_up,
    w_down,
):
    rows = tokens.shape[0]
    groups = lax.axis_size("exp")
    span = rows * groups
    seq_at = lax.axis_index("seq")
    exp_at = lax.axis_index("exp")
    z_hi, x_at, core = seq_at // 8, (seq_at // 2) % XS, seq_at % 2
    y_at, z_lo = exp_at // 2, exp_at % 2
    block_first = seq_at * span

    eighth = tokens.shape[1] // 8
    wq_t = jnp.transpose(w_query)
    wq_part = lax.dynamic_slice_in_dim(wq_t, (x_at * 2 + core) * eighth, eighth, 1)
    wq_part = jnp.concatenate(
        [lax.ppermute(wq_part, "exp", shift_y(-j)) for j in (1, 2, 3)], axis=0
    )

    pair_pos = block_first + y_at * (2 * rows) + jnp.concatenate(
        [z_lo * rows + jnp.arange(rows, dtype=jnp.int32), (1 - z_lo) * rows + jnp.arange(rows, dtype=jnp.int32)]
    )
    cosine, sine = angles(pair_pos)
    normed, piece = own_latents(
        tokens, attn_gain, w_latent, latent_gain, cosine[:rows], sine[:rows]
    )
    piece = jnp.concatenate([piece, lax.ppermute(piece, "exp", Z_LO)], axis=0)
    pieces = [piece] + [lax.ppermute(piece, "exp", shift_y(-j)) for j in (1, 2, 3)]
    pack = make_pack(pieces, w_expand)

    partner = lax.ppermute(normed, "exp", Z_LO)
    wq_parts = [wq_part] + [lax.ppermute(wq_part, "seq", shift_x(-j)) for j in (1, 2, 3)]
    wq_parts = wq_parts + [lax.ppermute(w, "seq", SIBLING) for w in wq_parts]
    normed, pack = lax.optimization_barrier((normed, pack))
    q_parts = make_queries(
        jnp.stack([x_at, core]).astype(jnp.int32), normed, partner, wq_t, wq_parts, cosine, sine
    )
    queries = [q_parts[0]] + [
        lax.ppermute(q_parts[(YS - j) % YS], "exp", shift_y(-j)) for j in (1, 2, 3)
    ]
    queries = jnp.concatenate(queries, axis=0)
    far_queries = lax.ppermute(queries, "seq", Z_DOWN)

    plus = lax.ppermute(pack, "seq", shift_x(-1))
    minus = lax.ppermute(pack, "seq", shift_x(1))
    far_a = lax.ppermute(plus[:UNIT], "seq", shift_x(-1))
    far_b = lax.ppermute(minus[UNIT:], "seq", shift_x(1))
    here = x_at * 2 + core
    stages, modes = [], []
    for held in ((( 0, pack),), ((1, plus), (3, minus)), ((2, far_a), (2, far_b))):
        stage, marks = [], []
        for j, mine in held:
            base = ((x_at + j) % XS) * 2
            stage += [mine, lax.ppermute(mine, "seq", SIBLING)]
            marks += [base + core, base + 1 - core]
        stages.append(stage)
        marks = jnp.stack(marks)
        modes.append(jnp.where(marks < here, 1, jnp.where(marks == here, 2, 0)))
    place = jnp.stack([y_at, z_lo, 1 - z_hi])
    carry = None
    for stage, causal in zip(stages, modes):
        marks = jnp.concatenate([jnp.where(z_hi == 0, 1, causal), place]).astype(jnp.int32)
        carry = attend(marks, (queries, far_queries), stage, carry, last=stage is stages[-1])
    first = carry
    far = lax.ppermute(first, "seq", Z_UP)
    second = attend(
        jnp.concatenate([jnp.where(z_hi == 0, jnp.concatenate(modes), 0), place]).astype(jnp.int32),
        (queries,), sum(stages, []), last=True,
    )
    attended = finish(jnp.stack([z_hi, y_at, z_lo]).astype(jnp.int32), first, far, second)
    by_head = lax.all_to_all(
        attended.reshape(groups, rows, VDIM), "exp", split_axis=0, concat_axis=0, tiled=True
    )

    half_o = w_output.shape[1] // 2
    wo_half = lax.dynamic_slice_in_dim(w_output, core * half_o, half_o, 1)
    wo_half, piece = lax.optimization_barrier((wo_half, piece))
    wo_half = jnp.concatenate([wo_half, lax.ppermute(wo_half, "exp", Z_LO)], axis=0)
    wo_half, queries = lax.optimization_barrier((wo_half, queries))
    shares = [wo_half] + [lax.ppermute(wo_half, "exp", shift_y(-j)) for j in (1, 2, 3)]
    *shares, first = lax.optimization_barrier((*shares, first))
    shares = shares + [lax.ppermute(w, "seq", SIBLING) for w in shares]
    steps = jnp.arange(groups, dtype=jnp.int32)
    near_first = ((y_at + steps // 2) % YS) * 2 + jnp.bitwise_xor(z_lo, steps % 2)

    picked = route_ids[:, :, None] == steps[None, None, :]
    picks = jnp.sum(picked.astype(jnp.int32), axis=1)
    weight = jnp.sum(jnp.where(picked, route_gates[:, :, None], 0.0), axis=1)
    slot = jnp.cumsum(picks, axis=0) - picks
    placed = (slot[:, :, None] == jnp.arange(CAP, dtype=jnp.int32)[None, None, :]) & (
        picks[:, :, None] > 0
    )
    gates = jnp.where(placed, weight[:, :, None], 0.0).reshape(rows, groups * CAP)
    chosen = jnp.transpose(placed.astype(jnp.bfloat16).reshape(rows, groups * CAP))

    mixed, outgoing = middle(
        jnp.concatenate([core[None], near_first]).astype(jnp.int32),
        by_head, shares, tokens, ffn_gain, chosen,
    )
    arrived = lax.all_to_all(outgoing, "exp", split_axis=0, concat_axis=0, tiled=True)
    result = expert(arrived, w_gate_up, w_down)
    returned = lax.all_to_all(result, "exp", split_axis=0, concat_axis=0, tiled=True)
    return combine(mixed, gates, returned)


def solution(mesh):
    placed = (
        P(("seq", "exp"), None),
        P(),
        P(None, "exp"),
        P(),
        P(),
        P(None, "exp"),
        P("exp", None),
        P(),
        P(("seq", "exp"), None),
        P(("seq", "exp"), None),
        P("exp", None, None),
        P("exp", None, None),
    )
    return jax.shard_map(
        body, mesh=mesh, in_specs=placed, out_specs=P(("seq", "exp"), None), check_vma=False
    )
```

```python
import functools

import jax
import jax.numpy as jnp
from jax import lax
from jax.experimental import pallas as pl
from jax.experimental.pallas import tpu as pltpu
from jax.sharding import PartitionSpec as P

FF = 1408
LATENT = 512
ROPE = 64
NOPE = 128
VDIM = 128
CAP = 64

EPS = 1e-06
UNIT = 1280
ROWS_BY_ROWS = (((1,), (1,)), ((), ()))
LOG2E = 1.4426950408889634
SCALE2 = (NOPE + ROPE) ** (-0.5) * LOG2E

XS, YS = 4, 4


def seq_perm(move):
    return [
        (z * 8 + x * 2 + c, move(z, x, c))
        for z in range(2) for x in range(XS) for c in range(2)
    ]


def shift_x(step):
    return seq_perm(lambda z, x, c: z * 8 + ((x + step) % XS) * 2 + c)


SIBLING = seq_perm(lambda z, x, c: z * 8 + x * 2 + 1 - c)
SWAP_X = seq_perm(lambda z, x, c: z * 8 + (x ^ 1) * 2 + c)
Z_DOWN = [(8 + t, t) for t in range(8)]
Z_UP = [(t, 8 + t) for t in range(8)]
Z_LO = [(e, e ^ 1) for e in range(8)]


def shift_y(step):
    return [(y * 2 + z, ((y + step) % YS) * 2 + z) for y in range(YS) for z in range(2)]


def scaled(values, gain):
    mean_sq = jnp.mean(values * values, axis=-1, keepdims=True)
    return values * lax.rsqrt(mean_sq + EPS) * gain


def angles(positions):
    half = ROPE // 2
    inverse = 10000.0 ** (-(jnp.arange(half, dtype=jnp.float32) * 2.0 / ROPE))
    theta = positions.astype(jnp.float32)[:, None] * inverse[None, :]
    return (jnp.cos(theta), jnp.sin(theta))


def rotate(values, cosine, sine):
    half = ROPE // 2
    first = values[..., :half]
    second = values[..., half:]
    return jnp.concatenate(
        [first * cosine - second * sine, second * cosine + first * sine], axis=-1
    )


def bring(sources, places, sems):
    copies = [
        pltpu.make_async_copy(source, place, sems.at[i])
        for i, (source, place) in enumerate(zip(sources, places))
    ]
    for copy in copies:
        copy.start()
    for copy in copies:
        copy.wait()


def latent_kernel(*refs):
    sources, (normed_out, piece_out), held, sems = refs[:6], refs[6:8], refs[8:14], refs[14]
    bring(sources, held, sems)
    tokens, gain, w_latent, latent_gain, cosine, sine = held
    resid = tokens[...].astype(jnp.float32)
    normed = scaled(resid, gain[...]).astype(jnp.bfloat16)
    normed_out[...] = normed
    mixed_kv = lax.dot_general(
        normed, w_latent[...], ROWS_BY_ROWS, preferred_element_type=jnp.float32
    )
    rows = tokens.shape[0]
    piece_out[:rows, :] = scaled(mixed_kv[:, :LATENT], latent_gain[...]).astype(jnp.bfloat16)
    ropes = rotate(mixed_kv[:, LATENT:], cosine[...], sine[...]).astype(jnp.bfloat16)
    for group in range(8):
        piece_out[rows:, group * ROPE:(group + 1) * ROPE] = ropes[group * 16:(group + 1) * 16, :]


def own_latents(tokens, gain, w_latent, latent_gain, cosine, sine):
    rows, width = tokens.shape
    vmem = pl.BlockSpec(memory_space=pltpu.VMEM)
    operands = (tokens, gain[None], jnp.transpose(w_latent), latent_gain[None], cosine, sine)
    return pl.pallas_call(
        latent_kernel,
        out_shape=(
            jax.ShapeDtypeStruct((rows, width), jnp.bfloat16),
            jax.ShapeDtypeStruct((rows + rows // 8, LATENT), jnp.bfloat16),
        ),
        in_specs=[pl.BlockSpec(memory_space=pltpu.HBM)] * 6,
        out_specs=(vmem, vmem),
        scratch_shapes=[pltpu.VMEM(x.shape, x.dtype) for x in operands]
        + [pltpu.SemaphoreType.DMA((6,))],
        compiler_params=pltpu.CompilerParams(vmem_limit_bytes=60 * 1024 * 1024),
        cost_estimate=pl.CostEstimate(
            flops=2 * rows * width * (LATENT + ROPE),
            bytes_accessed=2 * width * (LATENT + ROPE),
            transcendentals=0,
        ),
    )(*operands)


def pack_kernel(*refs):
    sources, out, held, sems = refs[:5], refs[5], refs[6:11], refs[11]
    bring(sources, held, sems)
    w_expand = held[4]
    for at in range(8):
        piece = held[at // 2]
        step = piece.shape[0] // 2
        rows = step * 8 // 9
        first = (at % 2) * step
        base, row = (at // 4) * UNIT, (at % 4) * rows
        expanded = jnp.dot(
            piece[first:first + rows, :], w_expand[...], preferred_element_type=jnp.float32
        ).astype(jnp.bfloat16)
        out[base + row:base + row + rows, :] = expanded[:, :NOPE]
        out[base + 4 * rows + row:base + 4 * rows + row + rows, :] = expanded[:, NOPE:]
        part = (at % 4) // 2
        for group in range(8):
            to = base + 8 * rows + (at % 2) * rows + group * 16
            out[to:to + 16, part * ROPE:(part + 1) * ROPE] = (
                piece[first + rows:first + step, group * ROPE:(group + 1) * ROPE]
            )


def make_pack(pieces, w_expand):
    operands = (*pieces, w_expand)
    return pl.pallas_call(
        pack_kernel,
        out_shape=jax.ShapeDtypeStruct((2 * UNIT, 128), jnp.bfloat16),
        in_specs=[pl.BlockSpec(memory_space=pltpu.HBM)] * 5,
        out_specs=pl.BlockSpec(memory_space=pltpu.VMEM),
        scratch_shapes=[pltpu.VMEM(x.shape, x.dtype) for x in operands]
        + [pltpu.SemaphoreType.DMA((5,))],
        compiler_params=pltpu.CompilerParams(vmem_limit_bytes=60 * 1024 * 1024),
        cost_estimate=pl.CostEstimate(
            flops=2 * 1024 * LATENT * 256, bytes_accessed=2 * 1024 * 1024, transcendentals=0
        ),
    )(*operands)


def query_kernel(place, *refs):
    sources, out, held, places, sems = refs[:9], refs[9], refs[10], refs[11:18], refs[18]
    rows, width = sources[0].shape
    places = [held.at[pl.ds(0, rows), :], held.at[pl.ds(rows, rows), :], *places]
    bring(sources, places, sems)
    w_own, weights, cosine, sine = places[2], places[3:7], places[7], places[8]
    chunk = width // 4
    others = 0.0
    for i, weight in enumerate(weights):
        at = ((place[0] + i) % 2) * 2 + (place[1] + i // 2) % 2
        others = others + lax.dot_general(
            held[:, pl.ds(pl.multiple_of(at * chunk, chunk), chunk)], weight[...],
            ROWS_BY_ROWS, preferred_element_type=jnp.float32,
        )
    size = NOPE + ROPE
    for j in range(YS):
        if j == 0:
            query = lax.dot_general(
                held[...], w_own[...], ROWS_BY_ROWS, preferred_element_type=jnp.float32
            )
        else:
            query = others[:, (j - 1) * size:j * size]
        head = (place[2] + j) % YS
        ropes = rotate(query[:, NOPE:], cosine[...], sine[...]).astype(jnp.bfloat16)
        out[head, :2 * rows, :] = query[:, :NOPE].astype(jnp.bfloat16)
        out[head, 2 * rows:, :] = jnp.concatenate([ropes[:rows], ropes[rows:]], axis=1)


def make_queries(place, own, partner, w_own, chunks, cosine, sine):
    rows, width = own.shape
    operands = (own, partner, w_own, *chunks, cosine, sine)
    return pl.pallas_call(
        query_kernel,
        out_shape=jax.ShapeDtypeStruct((YS, 3 * rows, 128), jnp.bfloat16),
        in_specs=[pl.BlockSpec(memory_space=pltpu.SMEM)]
        + [pl.BlockSpec(memory_space=pltpu.HBM)] * len(operands),
        out_specs=pl.BlockSpec(memory_space=pltpu.VMEM),
        scratch_shapes=[pltpu.VMEM((2 * rows, width), jnp.bfloat16)]
        + [pltpu.VMEM(x.shape, x.dtype) for x in operands[2:]]
        + [pltpu.SemaphoreType.DMA((len(operands),))],
        compiler_params=pltpu.CompilerParams(vmem_limit_bytes=28 * 1024 * 1024),
        cost_estimate=pl.CostEstimate(
            flops=4 * rows * width * 768, bytes_accessed=2 * width * 768, transcendentals=0
        ),
    )(place, *operands)


def attend_kernel(sizes, far, has_carry, last, sends, modes, *refs):
    count = len(sizes)
    q_refs, refs = refs[:1 + far], refs[1 + far:]
    packs, refs = refs[:count], refs[count:]
    q_held, held, query, q_sem, sems = refs[-5:]
    carry, refs = refs[:2 * has_carry], refs[2 * has_carry:-5]
    o_out, l_out = refs[0], refs[-1]
    rows = query.shape[0]
    packed, o_out = o_out, o_out.at[pl.ds(0, rows), :]
    part_rows = UNIT // 5
    units = [(i, at) for i in range(count) for at in range(sizes[i] // UNIT)]

    def q_copy(i):
        return pltpu.make_async_copy(q_refs[i], q_held, q_sem.at[0])

    def unit_copy(unit, i=0, at=0):
        place = held.at[pl.ds(pl.multiple_of(unit * UNIT, UNIT), UNIT), :]
        return pltpu.make_async_copy(packs[i].at[pl.ds(at * UNIT, UNIT), :], place, sems.at[unit])

    for i in range(1 + far):
        if far:
            pl.when(modes[count + 2] == i)(q_copy(i).start)
        else:
            q_copy(i).start()
    for unit, (i, at) in enumerate(units):
        pl.when(modes[i] != 0)(unit_copy(unit, i, at).start)
    if has_carry:
        o_out[...] = carry[0][...]
        l_out[...] = carry[1][...]
    else:
        o_out[...] = jnp.zeros_like(o_out)
        l_out[...] = jnp.zeros_like(l_out)
    q_copy(0).wait()

    some = part_rows // 2
    for piece in range(rows // part_rows):
        base = piece * 3 * some
        ropes = q_held[base + part_rows:base + 3 * some, :]
        for side in range(2):
            here = slice(piece * part_rows + side * some, piece * part_rows + (side + 1) * some)
            rope = ropes[:, side * ROPE:(side + 1) * ROPE]
            query[here, :NOPE] = q_held[base + side * some:base + (side + 1) * some, :]
            query[here, NOPE:] = jnp.concatenate([rope, rope], axis=1)

    def spot(unit, row, size=1):
        return pl.ds(pl.multiple_of(unit * UNIT + row * part_rows, part_rows), size * part_rows)

    def score(unit):
        nope = held[spot(unit, 0, 2), :]
        ropes = held[spot(unit, 4), :]
        left = lax.broadcasted_iota(jnp.int32, ropes.shape, 1) < ROPE
        none = jnp.zeros_like(ropes)
        ropes = jnp.concatenate([jnp.where(left, ropes, none), jnp.where(left, none, ropes)], axis=0)
        return lax.dot_general(
            query[...], jnp.concatenate([nope, ropes], axis=1), ROWS_BY_ROWS,
            preferred_element_type=jnp.float32,
        )

    def weigh(unit, diag=False):
        weights = jnp.exp2(score(unit) * SCALE2)
        if diag:
            q_pos = lax.broadcasted_iota(jnp.int32, weights.shape, 0)
            k_pos = lax.broadcasted_iota(jnp.int32, weights.shape, 1)
            k_pos = k_pos + (unit * 2 + modes[count]) * part_rows
            flip = modes[count + 1] * 128
            seen = ((k_pos & (rows - 1)) ^ flip) <= (q_pos ^ flip)
            weights = jnp.where(seen, weights, 0.0)
        total = l_out[...]
        for lane in range(2 * part_rows // 128):
            total = total + weights[:, lane * 128:(lane + 1) * 128]
        l_out[...] = total
        o_out[...] += jnp.dot(
            weights.astype(jnp.bfloat16), held[spot(unit, 2, 2), :],
            preferred_element_type=jnp.float32,
        )

    def visit(first, size, diag=False):
        chosen = [unit for unit, (i, _) in enumerate(units) if first <= i < first + size]
        for unit in chosen:
            unit_copy(unit).wait()
        for unit in chosen:
            weigh(unit, diag)

    if not has_carry:
        pl.when(modes[0] == 2)(functools.partial(visit, 0, 1, True))
        pl.when(modes[0] == 1)(functools.partial(visit, 0, 1))
        pl.when(modes[1] == 1)(functools.partial(visit, 1, 1))
    for i in range(0 if has_carry else 2, count, 2):
        pl.when(modes[i] == 1)(functools.partial(visit, i, 2))
    if last:
        lanes = lax.broadcasted_iota(jnp.int32, (128, 128), 1)
        sums = jnp.zeros((128, 128), jnp.float32)
        for group in range(rows // 128):
            total = jnp.sum(l_out[group * 128:(group + 1) * 128, :], axis=1, keepdims=True)
            sums = jnp.where(lanes == group, total, sums)
        packed[pl.ds(rows, 128), :] = sums
    if sends:
        away = refs[1]
        away[:rows, :] = o_out[...].astype(jnp.bfloat16)
        for term in range(3):
            part = sums.astype(jnp.bfloat16)
            away[rows + term * 128:rows + (term + 1) * 128, :] = part
            sums = sums - part.astype(jnp.float32)


def attend(modes, queries, packs, carry=None, last=False, sends=False):
    rows = 1024
    vmem = pl.BlockSpec(memory_space=pltpu.VMEM)
    sums = jax.ShapeDtypeStruct((rows, 128), jnp.float32)
    sizes = tuple(p.shape[0] for p in packs)
    scratch = [
        pltpu.VMEM(queries[0].shape, jnp.bfloat16),
        pltpu.VMEM((sum(sizes), 128), jnp.bfloat16),
        pltpu.VMEM((rows, 256), jnp.bfloat16),
        pltpu.SemaphoreType.DMA((1,)),
        pltpu.SemaphoreType.DMA((sum(sizes) // UNIT,)),
    ]
    if last:
        out = [jax.ShapeDtypeStruct((rows + 128, VDIM), jnp.float32)]
        if sends:
            out.append(jax.ShapeDtypeStruct((rows + 384, VDIM), jnp.bfloat16))
        scratch = [pltpu.VMEM((rows, 128), jnp.float32)] + scratch
    else:
        out = [sums, sums]
    extra = [] if carry is None else list(carry)
    keys = sum(sizes) // UNIT * 512
    anywhere = pl.BlockSpec(memory_space=pltpu.HBM)
    return pl.pallas_call(
        functools.partial(attend_kernel, sizes, len(queries) - 1, carry is not None, last, sends),
        out_shape=out,
        in_specs=[pl.BlockSpec(memory_space=pltpu.SMEM)]
        + [anywhere] * (len(queries) + len(packs)) + [vmem] * len(extra),
        out_specs=[vmem] * len(out),
        scratch_shapes=scratch,
        compiler_params=pltpu.CompilerParams(vmem_limit_bytes=28 * 1024 * 1024),
        cost_estimate=pl.CostEstimate(
            flops=rows * keys * 768, bytes_accessed=keys * 640, transcendentals=rows * keys
        ),
    )(modes, *queries, *packs, *extra)


def finish_kernel(flags, first, far, second, out):
    rows = 128
    count = out.shape[0] // rows
    kept = flags[0].astype(jnp.float32)
    lanes = lax.broadcasted_iota(jnp.int32, (rows, 128), 1)
    tail = count * rows
    totals = second[tail:tail + rows, :] + kept * first[tail:tail + rows, :]
    for term in range(3):
        totals = totals + kept * far[tail + term * rows:tail + (term + 1) * rows, :].astype(jnp.float32)
    for chunk in range(count):
        span = slice(chunk * rows, (chunk + 1) * rows)
        summed = second[span, :] + kept * (first[span, :] + far[span, :].astype(jnp.float32))
        total = jnp.sum(jnp.where(lanes == chunk, totals, 0.0), axis=1, keepdims=True)
        at = (chunk // 2 * 2 + ((chunk % 2) ^ flags[1])) * rows
        out[pl.ds(pl.multiple_of(at, rows), rows), :] = (summed / total).astype(jnp.bfloat16)


def finish(flags, first, far, second):
    vmem = pl.BlockSpec(memory_space=pltpu.VMEM)
    return pl.pallas_call(
        finish_kernel,
        out_shape=jax.ShapeDtypeStruct((first.shape[0] - 128, VDIM), jnp.bfloat16),
        in_specs=[pl.BlockSpec(memory_space=pltpu.SMEM)] + [vmem] * 3,
        out_specs=vmem,
        compiler_params=pltpu.CompilerParams(vmem_limit_bytes=8 * 1024 * 1024),
    )(flags, first, far, second)


def middle_kernel(flags, by_head, *refs):
    shares, refs = refs[:8], refs[8:]
    tokens, gain, chosen = refs[:3]
    mixed, out, held = refs[3:]
    rows, half = tokens.shape[0], shares[0].shape[1]
    for l in range(8):
        held[:, l * VDIM:(l + 1) * VDIM] = by_head[flags[1 + l]]
    for side in range(2):
        at = pl.multiple_of(jnp.where(flags[0] == side, 0, half), half)
        total = tokens[:, pl.ds(at, half)].astype(jnp.float32)
        for j in range(YS):
            total = total + jnp.dot(
                held[:, j * 256:(j + 1) * 256], shares[side * 4 + j][...],
                preferred_element_type=jnp.float32,
            )
        mixed[:, pl.ds(at, half)] = total
    normed = scaled(mixed[...], gain[...]).astype(jnp.bfloat16)
    for e in range(out.shape[0]):
        out[e] = jnp.dot(
            chosen[e * CAP:(e + 1) * CAP, :], normed, preferred_element_type=jnp.float32
        ).astype(jnp.bfloat16)


def middle(flags, by_head, shares, tokens, gain, chosen):
    rows, width = tokens.shape
    vmem = pl.BlockSpec(memory_space=pltpu.VMEM)
    return pl.pallas_call(
        middle_kernel,
        out_shape=(
            jax.ShapeDtypeStruct((rows, width), jnp.float32),
            jax.ShapeDtypeStruct((8, CAP, width), jnp.bfloat16),
        ),
        in_specs=[pl.BlockSpec(memory_space=pltpu.SMEM)] + [vmem] * 12,
        out_specs=(vmem,) * 2,
        scratch_shapes=[pltpu.VMEM((rows, 8 * VDIM), jnp.bfloat16)],
        compiler_params=pltpu.CompilerParams(vmem_limit_bytes=20 * 1024 * 1024),
        cost_estimate=pl.CostEstimate(
            flops=4 * rows * width * 1024, bytes_accessed=8 * width * 1024, transcendentals=0
        ),
    )(flags, by_head, *shares, tokens, gain[None], chosen)


FF_STEPS = FF // 128
DOWN_STEPS = 8


def expert_kernel(arrived, w_gate_up, w_down, out, gate_up, down, hidden, gate_sem, up_sem, down_sem):
    experts, items, width = arrived.shape
    cols = width // DOWN_STEPS

    def gate_copies(i):
        at = pl.ds(pl.multiple_of(i * 128, 128), 128)
        up = pl.ds(pl.multiple_of(FF + i * 128, 128), 128)
        return (
            pltpu.make_async_copy(w_gate_up.at[0, :, at], gate_up.at[:, at], gate_sem.at[i]),
            pltpu.make_async_copy(w_gate_up.at[0, :, up], gate_up.at[:, up], up_sem.at[i]),
        )

    def down_copy(i):
        at = pl.ds(pl.multiple_of(i * cols, cols), cols)
        return pltpu.make_async_copy(w_down.at[0, :, at], down.at[:, at], down_sem.at[i])

    for i in range(FF_STEPS):
        for copy in gate_copies(i):
            copy.start()
    for i in range(DOWN_STEPS):
        down_copy(i).start()
    rows = arrived[...].reshape(experts * items, width)

    def first(i, _):
        for copy in gate_copies(i):
            copy.wait()
        at = pl.ds(pl.multiple_of(i * 128, 128), 128)
        up = pl.ds(pl.multiple_of(FF + i * 128, 128), 128)
        both = jnp.concatenate([gate_up[:, at], gate_up[:, up]], axis=1)
        product = jnp.dot(rows, both, preferred_element_type=jnp.float32)
        hidden[:, at] = (jax.nn.silu(product[:, :128]) * product[:, 128:]).astype(jnp.bfloat16)
        return 0

    def second(i, _):
        down_copy(i).wait()
        at = pl.ds(pl.multiple_of(i * cols, cols), cols)
        result = jnp.dot(hidden[...], down[:, at], preferred_element_type=jnp.float32)
        out[:, :, at] = result.astype(jnp.bfloat16).reshape(experts, items, cols)
        return 0

    lax.fori_loop(0, FF_STEPS, first, 0)
    lax.fori_loop(0, DOWN_STEPS, second, 0)


def expert(arrived, w_gate_up, w_down):
    experts, items, width = arrived.shape
    vmem = pl.BlockSpec(memory_space=pltpu.VMEM)
    return pl.pallas_call(
        expert_kernel,
        out_shape=jax.ShapeDtypeStruct(arrived.shape, jnp.bfloat16),
        in_specs=[vmem, pl.BlockSpec(memory_space=pltpu.HBM), pl.BlockSpec(memory_space=pltpu.HBM)],
        out_specs=vmem,
        scratch_shapes=[
            pltpu.VMEM((width, 2 * FF), jnp.bfloat16),
            pltpu.VMEM((FF, width), jnp.bfloat16),
            pltpu.VMEM((experts * items, FF), jnp.bfloat16),
            pltpu.SemaphoreType.DMA((FF_STEPS,)),
            pltpu.SemaphoreType.DMA((FF_STEPS,)),
            pltpu.SemaphoreType.DMA((DOWN_STEPS,)),
        ],
        compiler_params=pltpu.CompilerParams(vmem_limit_bytes=48 * 1024 * 1024),
        cost_estimate=pl.CostEstimate(
            flops=6 * experts * items * width * FF, bytes_accessed=6 * width * FF, transcendentals=0
        ),
    )(arrived, w_gate_up, w_down)


def combine_kernel(mixed, gates, returned, out):
    rows = mixed.shape[0]
    first = gates[...].astype(jnp.bfloat16)
    rest = gates[...] - first.astype(jnp.float32)
    second = rest.astype(jnp.bfloat16)
    third = (rest - second.astype(jnp.float32)).astype(jnp.bfloat16)
    stacked = jnp.concatenate([first, second, third], axis=0)
    moe = jnp.dot(
        stacked, returned[...].reshape(gates.shape[1], mixed.shape[1]),
        preferred_element_type=jnp.float32,
    )
    moe = moe[:rows] + (moe[rows:2 * rows] + moe[2 * rows:])
    out[...] = (mixed[...] + moe).astype(jnp.bfloat16)


def combine(mixed, gates, returned):
    vmem = pl.BlockSpec(memory_space=pltpu.VMEM)
    return pl.pallas_call(
        combine_kernel,
        out_shape=jax.ShapeDtypeStruct(mixed.shape, jnp.bfloat16),
        in_specs=[vmem] * 3,
        out_specs=vmem,
        compiler_params=pltpu.CompilerParams(vmem_limit_bytes=24 * 1024 * 1024),
    )(mixed, gates, returned)


def body(
    tokens,
    attn_gain,
    w_query,
    w_latent,
    latent_gain,
    w_expand,
    w_output,
    ffn_gain,
    route_ids,
    route_gates,
    w_gate_up,
    w_down,
):
    rows = tokens.shape[0]
    groups = lax.axis_size("exp")
    span = rows * groups
    seq_at = lax.axis_index("seq")
    exp_at = lax.axis_index("exp")
    z_hi, x_at, core = seq_at // 8, (seq_at // 2) % XS, seq_at % 2
    y_at, z_lo = exp_at // 2, exp_at % 2
    block_first = seq_at * span

    own_pos = block_first + exp_at * rows + jnp.arange(rows, dtype=jnp.int32)
    own_cos, own_sin = angles(own_pos)
    normed, piece = own_latents(tokens, attn_gain, w_latent, latent_gain, own_cos, own_sin)
    partner_pos = block_first + jnp.bitwise_xor(exp_at, 1) * rows + jnp.arange(rows, dtype=jnp.int32)
    partner_pos, piece = lax.optimization_barrier((partner_pos, piece))
    partner_cos, partner_sin = angles(partner_pos)
    cosine = jnp.concatenate([own_cos, partner_cos], axis=0)
    sine = jnp.concatenate([own_sin, partner_sin], axis=0)
    quarter = tokens.shape[1] // 4
    wq_t = jnp.transpose(w_query)
    wq_part = lax.dynamic_slice_in_dim(wq_t, ((x_at % 2) * 2 + core) * quarter, quarter, 1)
    wq_part, piece = lax.optimization_barrier((wq_part, piece))
    wq_part = jnp.concatenate(
        [lax.ppermute(wq_part, "exp", shift_y(-j)) for j in (1, 2, 3)], axis=0
    )
    piece = jnp.concatenate([piece, lax.ppermute(piece, "exp", Z_LO)], axis=0)
    pieces = [piece] + [lax.ppermute(piece, "exp", shift_y(-j)) for j in (1, 2, 3)]

    normed, piece = lax.optimization_barrier((normed, piece))
    partner = lax.ppermute(normed, "exp", Z_LO)
    wq_parts = [wq_part, lax.ppermute(wq_part, "seq", SWAP_X)]
    wq_parts = wq_parts + [lax.ppermute(w, "seq", SIBLING) for w in wq_parts]
    pack = make_pack(pieces, w_expand)
    normed, pack = lax.optimization_barrier((normed, pack))
    q_parts = make_queries(
        jnp.stack([x_at, core, y_at]).astype(jnp.int32), normed, partner, wq_t, wq_parts, cosine, sine
    )
    same_z = [[y * 2 + z for y in range(YS)] for z in range(2)]
    queries = lax.all_to_all(
        q_parts, "exp", split_axis=0, concat_axis=0, axis_index_groups=same_z, tiled=True
    ).reshape(-1, 128)
    plus = lax.ppermute(pack, "seq", shift_x(-1))
    minus = lax.ppermute(pack, "seq", shift_x(1))
    queries, half_a, half_b = lax.optimization_barrier((queries, plus[:UNIT], minus[UNIT:]))
    far_queries = lax.ppermute(queries, "seq", Z_DOWN)
    heads_queries = queries
    far_a = lax.ppermute(half_a, "seq", shift_x(-1))
    far_b = lax.ppermute(half_b, "seq", shift_x(1))
    here = x_at * 2 + core
    stages, modes = [], []
    for held in (((0, pack), (1, plus), (3, minus)), ((2, far_a), (2, far_b))):
        stage, marks = [], []
        for j, mine in held:
            base = ((x_at + j) % XS) * 2
            stage += [mine, lax.ppermute(mine, "seq", SIBLING)]
            marks += [base + core, base + 1 - core]
        stages.append(stage)
        marks = jnp.stack(marks)
        modes.append(jnp.where(marks < here, 1, jnp.where(marks == here, 2, 0)))
    place = jnp.stack([y_at, z_lo, 1 - z_hi])
    carry = None
    for stage, causal in zip(stages, modes):
        marks = jnp.concatenate([jnp.where(z_hi == 0, 1, causal), place]).astype(jnp.int32)
        final = stage is stages[-1]
        carry = attend(marks, (queries, far_queries), stage, carry, last=final, sends=final)
    first, away = carry
    far = lax.ppermute(away, "seq", Z_UP)
    carry = None
    queries, first = lax.optimization_barrier((queries, first))
    for stage, causal in zip(stages, modes):
        marks = jnp.concatenate([jnp.where(z_hi == 0, causal, 0), place]).astype(jnp.int32)
        if carry is not None:
            early = carry[0]
        carry = attend(marks, (queries,), stage, carry, last=stage is stages[-1])
    second, = carry
    attended = finish(jnp.stack([z_hi, z_lo]).astype(jnp.int32), first, far, second)
    by_head = lax.all_to_all(
        attended.reshape(groups, rows, VDIM), "exp", split_axis=0, concat_axis=0, tiled=True
    )

    half_o = w_output.shape[1] // 2
    wo_half = lax.dynamic_slice_in_dim(w_output, core * half_o, half_o, 1)
    wo_half, partner = lax.optimization_barrier((wo_half, partner))
    wo_half = jnp.concatenate([wo_half, lax.ppermute(wo_half, "exp", Z_LO)], axis=0)
    wo_half, heads_queries = lax.optimization_barrier((wo_half, heads_queries))
    shares = [wo_half] + [lax.ppermute(wo_half, "exp", shift_y(-j)) for j in (1, 2, 3)]
    *shares, early = lax.optimization_barrier((*shares, early))
    shares = shares + [lax.ppermute(w, "seq", SIBLING) for w in shares]
    steps = jnp.arange(groups, dtype=jnp.int32)
    near_first = ((y_at + steps // 2) % YS) * 2 + jnp.bitwise_xor(z_lo, steps % 2)

    picked = route_ids[:, :, None] == steps[None, None, :]
    picks = jnp.sum(picked.astype(jnp.int32), axis=1)
    weight = jnp.sum(jnp.where(picked, route_gates[:, :, None], 0.0), axis=1)
    slot = jnp.cumsum(picks, axis=0) - picks
    placed = (slot[:, :, None] == jnp.arange(CAP, dtype=jnp.int32)[None, None, :]) & (
        picks[:, :, None] > 0
    )
    gates = jnp.where(placed, weight[:, :, None], 0.0).reshape(rows, groups * CAP)
    chosen = jnp.transpose(placed.astype(jnp.bfloat16).reshape(rows, groups * CAP))

    mixed, outgoing = middle(
        jnp.concatenate([core[None], near_first]).astype(jnp.int32),
        by_head, shares, tokens, ffn_gain, chosen,
    )
    arrived = lax.all_to_all(outgoing, "exp", split_axis=0, concat_axis=0, tiled=True)
    result = expert(arrived, w_gate_up, w_down)
    returned = lax.all_to_all(result, "exp", split_axis=0, concat_axis=0, tiled=True)
    return combine(mixed, gates, returned)


def solution(mesh):
    placed = (
        P(("seq", "exp"), None),
        P(),
        P(None, "exp"),
        P(),
        P(),
        P(None, "exp"),
        P("exp", None),
        P(),
        P(("seq", "exp"), None),
        P(("seq", "exp"), None),
        P("exp", None, None),
        P("exp", None, None),
    )
    return jax.shard_map(
        body, mesh=mesh, in_specs=placed, out_specs=P(("seq", "exp"), None), check_vma=False
    )
```

```python
import functools

import jax
import jax.numpy as jnp
from jax import lax
from jax.experimental import pallas as pl
from jax.experimental.pallas import tpu as pltpu
from jax.sharding import PartitionSpec as P

FF = 1408
LATENT = 512
ROPE = 64
NOPE = 128
VDIM = 128
CAP = 64

EPS = 1e-06
UNIT = 1280
ROWS_BY_ROWS = (((1,), (1,)), ((), ()))
LOG2E = 1.4426950408889634
SCALE2 = (NOPE + ROPE) ** (-0.5) * LOG2E

XS, YS = 4, 4


def seq_perm(move):
    return [
        (z * 8 + x * 2 + c, move(z, x, c))
        for z in range(2) for x in range(XS) for c in range(2)
    ]


def shift_x(step):
    return seq_perm(lambda z, x, c: z * 8 + ((x + step) % XS) * 2 + c)


SIBLING = seq_perm(lambda z, x, c: z * 8 + x * 2 + 1 - c)
SWAP_X = seq_perm(lambda z, x, c: z * 8 + (x ^ 1) * 2 + c)
Z_DOWN = [(8 + t, t) for t in range(8)]
Z_UP = [(t, 8 + t) for t in range(8)]
Z_LO = [(e, e ^ 1) for e in range(8)]


def shift_y(step):
    return [(y * 2 + z, ((y + step) % YS) * 2 + z) for y in range(YS) for z in range(2)]


def scaled(values, gain):
    mean_sq = jnp.mean(values * values, axis=-1, keepdims=True)
    return values * lax.rsqrt(mean_sq + EPS) * gain


def angles(positions):
    half = ROPE // 2
    inverse = 10000.0 ** (-(jnp.arange(half, dtype=jnp.float32) * 2.0 / ROPE))
    theta = positions.astype(jnp.float32)[:, None] * inverse[None, :]
    return (jnp.cos(theta), jnp.sin(theta))


def rotate(values, cosine, sine):
    half = ROPE // 2
    first = values[..., :half]
    second = values[..., half:]
    return jnp.concatenate(
        [first * cosine - second * sine, second * cosine + first * sine], axis=-1
    )


def bring(sources, places, sems):
    copies = [
        pltpu.make_async_copy(source, place, sems.at[i])
        for i, (source, place) in enumerate(zip(sources, places))
    ]
    for copy in copies:
        copy.start()
    for copy in copies:
        copy.wait()


def latent_kernel(*refs):
    sources, (normed_out, piece_out), held, sems = refs[:6], refs[6:8], refs[8:14], refs[14]
    bring(sources, held, sems)
    tokens, gain, w_latent, latent_gain, cosine, sine = held
    resid = tokens[...].astype(jnp.float32)
    normed = scaled(resid, gain[...]).astype(jnp.bfloat16)
    normed_out[...] = normed
    mixed_kv = lax.dot_general(
        normed, w_latent[...], ROWS_BY_ROWS, preferred_element_type=jnp.float32
    )
    rows = tokens.shape[0]
    piece_out[:rows, :] = scaled(mixed_kv[:, :LATENT], latent_gain[...]).astype(jnp.bfloat16)
    ropes = rotate(mixed_kv[:, LATENT:], cosine[...], sine[...]).astype(jnp.bfloat16)
    for group in range(8):
        piece_out[rows:, group * ROPE:(group + 1) * ROPE] = ropes[group * 16:(group + 1) * 16, :]


def own_latents(tokens, gain, w_latent, latent_gain, cosine, sine):
    rows, width = tokens.shape
    vmem = pl.BlockSpec(memory_space=pltpu.VMEM)
    operands = (tokens, gain[None], jnp.transpose(w_latent), latent_gain[None], cosine, sine)
    return pl.pallas_call(
        latent_kernel,
        out_shape=(
            jax.ShapeDtypeStruct((rows, width), jnp.bfloat16),
            jax.ShapeDtypeStruct((rows + rows // 8, LATENT), jnp.bfloat16),
        ),
        in_specs=[pl.BlockSpec(memory_space=pltpu.HBM)] * 6,
        out_specs=(vmem, vmem),
        scratch_shapes=[pltpu.VMEM(x.shape, x.dtype) for x in operands]
        + [pltpu.SemaphoreType.DMA((6,))],
        compiler_params=pltpu.CompilerParams(vmem_limit_bytes=60 * 1024 * 1024),
        cost_estimate=pl.CostEstimate(
            flops=2 * rows * width * (LATENT + ROPE),
            bytes_accessed=2 * width * (LATENT + ROPE),
            transcendentals=0,
        ),
    )(*operands)


def pack_kernel(*refs):
    sources, out, held, sems = refs[:5], refs[5], refs[6:11], refs[11]
    bring(sources, held, sems)
    w_expand = held[4]
    for at in range(8):
        piece = held[at // 2]
        step = piece.shape[0] // 2
        rows = step * 8 // 9
        first = (at % 2) * step
        base, row = (at // 4) * UNIT, (at % 4) * rows
        expanded = jnp.dot(
            piece[first:first + rows, :], w_expand[...], preferred_element_type=jnp.float32
        ).astype(jnp.bfloat16)
        out[base + row:base + row + rows, :] = expanded[:, :NOPE]
        out[base + 4 * rows + row:base + 4 * rows + row + rows, :] = expanded[:, NOPE:]
        part = (at % 4) // 2
        for group in range(8):
            to = base + 8 * rows + (at % 2) * rows + group * 16
            out[to:to + 16, part * ROPE:(part + 1) * ROPE] = (
                piece[first + rows:first + step, group * ROPE:(group + 1) * ROPE]
            )


def make_pack(pieces, w_expand):
    operands = (*pieces, w_expand)
    return pl.pallas_call(
        pack_kernel,
        out_shape=jax.ShapeDtypeStruct((2 * UNIT, 128), jnp.bfloat16),
        in_specs=[pl.BlockSpec(memory_space=pltpu.HBM)] * 5,
        out_specs=pl.BlockSpec(memory_space=pltpu.VMEM),
        scratch_shapes=[pltpu.VMEM(x.shape, x.dtype) for x in operands]
        + [pltpu.SemaphoreType.DMA((5,))],
        compiler_params=pltpu.CompilerParams(vmem_limit_bytes=60 * 1024 * 1024),
        cost_estimate=pl.CostEstimate(
            flops=2 * 1024 * LATENT * 256, bytes_accessed=2 * 1024 * 1024, transcendentals=0
        ),
    )(*operands)


def query_kernel(place, *refs):
    sources, out, held, places, sems = refs[:9], refs[9], refs[10], refs[11:18], refs[18]
    rows, width = sources[0].shape
    places = [held.at[pl.ds(0, rows), :], held.at[pl.ds(rows, rows), :], *places]
    bring(sources, places, sems)
    w_own, weights, cosine, sine = places[2], places[3:7], places[7], places[8]
    chunk = width // 4
    others = 0.0
    for i, weight in enumerate(weights):
        at = ((place[0] + i) % 2) * 2 + (place[1] + i // 2) % 2
        others = others + lax.dot_general(
            held[:, pl.ds(pl.multiple_of(at * chunk, chunk), chunk)], weight[...],
            ROWS_BY_ROWS, preferred_element_type=jnp.float32,
        )
    size = NOPE + ROPE
    for j in range(YS):
        if j == 0:
            query = lax.dot_general(
                held[...], w_own[...], ROWS_BY_ROWS, preferred_element_type=jnp.float32
            )
        else:
            query = others[:, (j - 1) * size:j * size]
        head = (place[2] + j) % YS
        ropes = rotate(query[:, NOPE:], cosine[...], sine[...]).astype(jnp.bfloat16)
        out[head, :2 * rows, :] = query[:, :NOPE].astype(jnp.bfloat16)
        out[head, 2 * rows:, :] = jnp.concatenate([ropes[:rows], ropes[rows:]], axis=1)


def make_queries(place, own, partner, w_own, chunks, cosine, sine):
    rows, width = own.shape
    operands = (own, partner, w_own, *chunks, cosine, sine)
    return pl.pallas_call(
        query_kernel,
        out_shape=jax.ShapeDtypeStruct((YS, 3 * rows, 128), jnp.bfloat16),
        in_specs=[pl.BlockSpec(memory_space=pltpu.SMEM)]
        + [pl.BlockSpec(memory_space=pltpu.HBM)] * len(operands),
        out_specs=pl.BlockSpec(memory_space=pltpu.VMEM),
        scratch_shapes=[pltpu.VMEM((2 * rows, width), jnp.bfloat16)]
        + [pltpu.VMEM(x.shape, x.dtype) for x in operands[2:]]
        + [pltpu.SemaphoreType.DMA((len(operands),))],
        compiler_params=pltpu.CompilerParams(vmem_limit_bytes=28 * 1024 * 1024),
        cost_estimate=pl.CostEstimate(
            flops=4 * rows * width * 768, bytes_accessed=2 * width * 768, transcendentals=0
        ),
    )(place, *operands)


def attend_kernel(sizes, far, has_carry, last, sends, modes, *refs):
    count = len(sizes)
    q_refs, refs = refs[:1 + far], refs[1 + far:]
    packs, refs = refs[:count], refs[count:]
    q_held, held, query, q_sem, sems = refs[-5:]
    carry, refs = refs[:2 * has_carry], refs[2 * has_carry:-5]
    o_out, l_out = refs[0], refs[-1]
    rows = query.shape[0]
    packed, o_out = o_out, o_out.at[pl.ds(0, rows), :]
    part_rows = UNIT // 5
    units = [(i, at) for i in range(count) for at in range(sizes[i] // UNIT)]

    def q_copy(i):
        return pltpu.make_async_copy(q_refs[i], q_held, q_sem.at[0])

    def unit_copy(unit, i=0, at=0):
        place = held.at[pl.ds(pl.multiple_of(unit * UNIT, UNIT), UNIT), :]
        return pltpu.make_async_copy(packs[i].at[pl.ds(at * UNIT, UNIT), :], place, sems.at[unit])

    for i in range(1 + far):
        if far:
            pl.when(modes[count + 2] == i)(q_copy(i).start)
        else:
            q_copy(i).start()
    for unit, (i, at) in enumerate(units):
        pl.when(modes[i] != 0)(unit_copy(unit, i, at).start)
    if has_carry:
        o_out[...] = carry[0][...]
        l_out[...] = carry[1][...]
    else:
        o_out[...] = jnp.zeros_like(o_out)
        l_out[...] = jnp.zeros_like(l_out)
    q_copy(0).wait()

    some = part_rows // 2
    for piece in range(rows // part_rows):
        base = piece * 3 * some
        ropes = q_held[base + part_rows:base + 3 * some, :]
        for side in range(2):
            here = slice(piece * part_rows + side * some, piece * part_rows + (side + 1) * some)
            rope = ropes[:, side * ROPE:(side + 1) * ROPE]
            query[here, :NOPE] = q_held[base + side * some:base + (side + 1) * some, :]
            query[here, NOPE:] = jnp.concatenate([rope, rope], axis=1)

    def spot(unit, row, size=1):
        return pl.ds(pl.multiple_of(unit * UNIT + row * part_rows, part_rows), size * part_rows)

    def score(unit):
        nope = held[spot(unit, 0, 2), :]
        ropes = held[spot(unit, 4), :]
        left = lax.broadcasted_iota(jnp.int32, ropes.shape, 1) < ROPE
        none = jnp.zeros_like(ropes)
        ropes = jnp.concatenate([jnp.where(left, ropes, none), jnp.where(left, none, ropes)], axis=0)
        return lax.dot_general(
            query[...], jnp.concatenate([nope, ropes], axis=1), ROWS_BY_ROWS,
            preferred_element_type=jnp.float32,
        )

    def weigh(unit, diag=False):
        weights = jnp.exp2(score(unit) * SCALE2)
        if diag:
            q_pos = lax.broadcasted_iota(jnp.int32, weights.shape, 0)
            k_pos = lax.broadcasted_iota(jnp.int32, weights.shape, 1)
            k_pos = k_pos + (unit * 2 + modes[count]) * part_rows
            flip = modes[count + 1] * 128
            seen = ((k_pos & (rows - 1)) ^ flip) <= (q_pos ^ flip)
            weights = jnp.where(seen, weights, 0.0)
        total = l_out[...]
        for lane in range(2 * part_rows // 128):
            total = total + weights[:, lane * 128:(lane + 1) * 128]
        l_out[...] = total
        o_out[...] += jnp.dot(
            weights.astype(jnp.bfloat16), held[spot(unit, 2, 2), :],
            preferred_element_type=jnp.float32,
        )

    def visit(first, size, diag=False):
        chosen = [unit for unit, (i, _) in enumerate(units) if first <= i < first + size]
        for unit in chosen:
            unit_copy(unit).wait()
        for unit in chosen:
            weigh(unit, diag)

    if not has_carry:
        pl.when(modes[0] == 2)(functools.partial(visit, 0, 1, True))
        pl.when(modes[0] == 1)(functools.partial(visit, 0, 1))
        pl.when(modes[1] == 1)(functools.partial(visit, 1, 1))
    for i in range(0 if has_carry else 2, count, 2):
        pl.when(modes[i] == 1)(functools.partial(visit, i, 2))
    if last:
        lanes = lax.broadcasted_iota(jnp.int32, (128, 128), 1)
        sums = jnp.zeros((128, 128), jnp.float32)
        for group in range(rows // 128):
            total = jnp.sum(l_out[group * 128:(group + 1) * 128, :], axis=1, keepdims=True)
            sums = jnp.where(lanes == group, total, sums)
        packed[pl.ds(rows, 128), :] = sums
    if sends:
        away = refs[1]
        away[:rows, :] = o_out[...].astype(jnp.bfloat16)
        for term in range(3):
            part = sums.astype(jnp.bfloat16)
            away[rows + term * 128:rows + (term + 1) * 128, :] = part
            sums = sums - part.astype(jnp.float32)


def attend(modes, queries, packs, carry=None, last=False, sends=False):
    rows = 1024
    vmem = pl.BlockSpec(memory_space=pltpu.VMEM)
    sums = jax.ShapeDtypeStruct((rows, 128), jnp.float32)
    sizes = tuple(p.shape[0] for p in packs)
    scratch = [
        pltpu.VMEM(queries[0].shape, jnp.bfloat16),
        pltpu.VMEM((sum(sizes), 128), jnp.bfloat16),
        pltpu.VMEM((rows, 256), jnp.bfloat16),
        pltpu.SemaphoreType.DMA((1,)),
        pltpu.SemaphoreType.DMA((sum(sizes) // UNIT,)),
    ]
    if last:
        out = [jax.ShapeDtypeStruct((rows + 128, VDIM), jnp.float32)]
        if sends:
            out.append(jax.ShapeDtypeStruct((rows + 384, VDIM), jnp.bfloat16))
        scratch = [pltpu.VMEM((rows, 128), jnp.float32)] + scratch
    else:
        out = [sums, sums]
    extra = [] if carry is None else list(carry)
    keys = sum(sizes) // UNIT * 512
    anywhere = pl.BlockSpec(memory_space=pltpu.HBM)
    return pl.pallas_call(
        functools.partial(attend_kernel, sizes, len(queries) - 1, carry is not None, last, sends),
        out_shape=out,
        in_specs=[pl.BlockSpec(memory_space=pltpu.SMEM)]
        + [anywhere] * (len(queries) + len(packs)) + [vmem] * len(extra),
        out_specs=[vmem] * len(out),
        scratch_shapes=scratch,
        compiler_params=pltpu.CompilerParams(vmem_limit_bytes=28 * 1024 * 1024),
        cost_estimate=pl.CostEstimate(
            flops=rows * keys * 768, bytes_accessed=keys * 640, transcendentals=rows * keys
        ),
    )(modes, *queries, *packs, *extra)


def finish_kernel(flags, first, far, second, out):
    rows = 128
    count = out.shape[0] // rows
    kept = flags[0].astype(jnp.float32)
    lanes = lax.broadcasted_iota(jnp.int32, (rows, 128), 1)
    tail = count * rows
    totals = second[tail:tail + rows, :] + kept * first[tail:tail + rows, :]
    for term in range(3):
        totals = totals + kept * far[tail + term * rows:tail + (term + 1) * rows, :].astype(jnp.float32)
    for chunk in range(count):
        span = slice(chunk * rows, (chunk + 1) * rows)
        summed = second[span, :] + kept * (first[span, :] + far[span, :].astype(jnp.float32))
        total = jnp.sum(jnp.where(lanes == chunk, totals, 0.0), axis=1, keepdims=True)
        at = (chunk // 2 * 2 + ((chunk % 2) ^ flags[1])) * rows
        out[pl.ds(pl.multiple_of(at, rows), rows), :] = (summed / total).astype(jnp.bfloat16)


def finish(flags, first, far, second):
    vmem = pl.BlockSpec(memory_space=pltpu.VMEM)
    return pl.pallas_call(
        finish_kernel,
        out_shape=jax.ShapeDtypeStruct((first.shape[0] - 128, VDIM), jnp.bfloat16),
        in_specs=[pl.BlockSpec(memory_space=pltpu.SMEM)] + [vmem] * 3,
        out_specs=vmem,
        compiler_params=pltpu.CompilerParams(vmem_limit_bytes=8 * 1024 * 1024),
    )(flags, first, far, second)


def middle_kernel(flags, by_head, *refs):
    shares, refs = refs[:8], refs[8:]
    tokens, gain, chosen = refs[:3]
    mixed, out, held = refs[3:]
    rows, half = tokens.shape[0], shares[0].shape[1]
    for l in range(8):
        held[:, l * VDIM:(l + 1) * VDIM] = by_head[flags[1 + l]]
    for side in range(2):
        at = pl.multiple_of(jnp.where(flags[0] == side, 0, half), half)
        total = tokens[:, pl.ds(at, half)].astype(jnp.float32)
        for j in range(YS):
            total = total + jnp.dot(
                held[:, j * 256:(j + 1) * 256], shares[side * 4 + j][...],
                preferred_element_type=jnp.float32,
            )
        mixed[:, pl.ds(at, half)] = total
    normed = scaled(mixed[...], gain[...]).astype(jnp.bfloat16)
    for e in range(out.shape[0]):
        out[e] = jnp.dot(
            chosen[e * CAP:(e + 1) * CAP, :], normed, preferred_element_type=jnp.float32
        ).astype(jnp.bfloat16)


def middle(flags, by_head, shares, tokens, gain, chosen):
    rows, width = tokens.shape
    vmem = pl.BlockSpec(memory_space=pltpu.VMEM)
    return pl.pallas_call(
        middle_kernel,
        out_shape=(
            jax.ShapeDtypeStruct((rows, width), jnp.float32),
            jax.ShapeDtypeStruct((8, CAP, width), jnp.bfloat16),
        ),
        in_specs=[pl.BlockSpec(memory_space=pltpu.SMEM)] + [vmem] * 12,
        out_specs=(vmem,) * 2,
        scratch_shapes=[pltpu.VMEM((rows, 8 * VDIM), jnp.bfloat16)],
        compiler_params=pltpu.CompilerParams(vmem_limit_bytes=20 * 1024 * 1024),
        cost_estimate=pl.CostEstimate(
            flops=4 * rows * width * 1024, bytes_accessed=8 * width * 1024, transcendentals=0
        ),
    )(flags, by_head, *shares, tokens, gain[None], chosen)


FF_STEPS = FF // 128
DOWN_STEPS = 8


def expert_kernel(arrived, w_gate_up, w_down, out, gate_up, down, hidden, gate_sem, up_sem, down_sem):
    experts, items, width = arrived.shape
    cols = width // DOWN_STEPS

    def gate_copies(i):
        at = pl.ds(pl.multiple_of(i * 128, 128), 128)
        up = pl.ds(pl.multiple_of(FF + i * 128, 128), 128)
        return (
            pltpu.make_async_copy(w_gate_up.at[0, :, at], gate_up.at[:, at], gate_sem.at[i]),
            pltpu.make_async_copy(w_gate_up.at[0, :, up], gate_up.at[:, up], up_sem.at[i]),
        )

    def down_copy(i):
        at = pl.ds(pl.multiple_of(i * cols, cols), cols)
        return pltpu.make_async_copy(w_down.at[0, :, at], down.at[:, at], down_sem.at[i])

    for i in range(FF_STEPS):
        for copy in gate_copies(i):
            copy.start()
    for i in range(DOWN_STEPS):
        down_copy(i).start()
    rows = arrived[...].reshape(experts * items, width)

    def first(i, _):
        for copy in gate_copies(i):
            copy.wait()
        at = pl.ds(pl.multiple_of(i * 128, 128), 128)
        up = pl.ds(pl.multiple_of(FF + i * 128, 128), 128)
        both = jnp.concatenate([gate_up[:, at], gate_up[:, up]], axis=1)
        product = jnp.dot(rows, both, preferred_element_type=jnp.float32)
        hidden[:, at] = (jax.nn.silu(product[:, :128]) * product[:, 128:]).astype(jnp.bfloat16)
        return 0

    def second(i, _):
        down_copy(i).wait()
        at = pl.ds(pl.multiple_of(i * cols, cols), cols)
        result = jnp.dot(hidden[...], down[:, at], preferred_element_type=jnp.float32)
        out[:, :, at] = result.astype(jnp.bfloat16).reshape(experts, items, cols)
        return 0

    lax.fori_loop(0, FF_STEPS, first, 0)
    lax.fori_loop(0, DOWN_STEPS, second, 0)


def expert(arrived, w_gate_up, w_down):
    experts, items, width = arrived.shape
    vmem = pl.BlockSpec(memory_space=pltpu.VMEM)
    return pl.pallas_call(
        expert_kernel,
        out_shape=jax.ShapeDtypeStruct(arrived.shape, jnp.bfloat16),
        in_specs=[vmem, pl.BlockSpec(memory_space=pltpu.HBM), pl.BlockSpec(memory_space=pltpu.HBM)],
        out_specs=vmem,
        scratch_shapes=[
            pltpu.VMEM((width, 2 * FF), jnp.bfloat16),
            pltpu.VMEM((FF, width), jnp.bfloat16),
            pltpu.VMEM((experts * items, FF), jnp.bfloat16),
            pltpu.SemaphoreType.DMA((FF_STEPS,)),
            pltpu.SemaphoreType.DMA((FF_STEPS,)),
            pltpu.SemaphoreType.DMA((DOWN_STEPS,)),
        ],
        compiler_params=pltpu.CompilerParams(vmem_limit_bytes=48 * 1024 * 1024),
        cost_estimate=pl.CostEstimate(
            flops=6 * experts * items * width * FF, bytes_accessed=6 * width * FF, transcendentals=0
        ),
    )(arrived, w_gate_up, w_down)


def combine_kernel(mixed, gates, returned, out):
    rows = mixed.shape[0]
    first = gates[...].astype(jnp.bfloat16)
    rest = gates[...] - first.astype(jnp.float32)
    second = rest.astype(jnp.bfloat16)
    third = (rest - second.astype(jnp.float32)).astype(jnp.bfloat16)
    stacked = jnp.concatenate([first, second, third], axis=0)
    moe = jnp.dot(
        stacked, returned[...].reshape(gates.shape[1], mixed.shape[1]),
        preferred_element_type=jnp.float32,
    )
    moe = moe[:rows] + (moe[rows:2 * rows] + moe[2 * rows:])
    out[...] = (mixed[...] + moe).astype(jnp.bfloat16)


def combine(mixed, gates, returned):
    vmem = pl.BlockSpec(memory_space=pltpu.VMEM)
    return pl.pallas_call(
        combine_kernel,
        out_shape=jax.ShapeDtypeStruct(mixed.shape, jnp.bfloat16),
        in_specs=[vmem] * 3,
        out_specs=vmem,
        compiler_params=pltpu.CompilerParams(vmem_limit_bytes=24 * 1024 * 1024),
    )(mixed, gates, returned)


def body(
    tokens,
    attn_gain,
    w_query,
    w_latent,
    latent_gain,
    w_expand,
    w_output,
    ffn_gain,
    route_ids,
    route_gates,
    w_gate_up,
    w_down,
):
    rows = tokens.shape[0]
    groups = lax.axis_size("exp")
    span = rows * groups
    seq_at = lax.axis_index("seq")
    exp_at = lax.axis_index("exp")
    z_hi, x_at, core = seq_at // 8, (seq_at // 2) % XS, seq_at % 2
    y_at, z_lo = exp_at // 2, exp_at % 2
    block_first = seq_at * span

    own_pos = block_first + exp_at * rows + jnp.arange(rows, dtype=jnp.int32)
    own_cos, own_sin = angles(own_pos)
    normed, piece = own_latents(tokens, attn_gain, w_latent, latent_gain, own_cos, own_sin)
    partner_pos = block_first + jnp.bitwise_xor(exp_at, 1) * rows + jnp.arange(rows, dtype=jnp.int32)
    partner_pos, piece = lax.optimization_barrier((partner_pos, piece))
    partner_cos, partner_sin = angles(partner_pos)
    cosine = jnp.concatenate([own_cos, partner_cos], axis=0)
    sine = jnp.concatenate([own_sin, partner_sin], axis=0)
    quarter = tokens.shape[1] // 4
    wq_t = jnp.transpose(w_query)
    wq_part = lax.dynamic_slice_in_dim(wq_t, ((x_at % 2) * 2 + core) * quarter, quarter, 1)
    wq_part, piece = lax.optimization_barrier((wq_part, piece))
    wq_part = jnp.concatenate(
        [lax.ppermute(wq_part, "exp", shift_y(-j)) for j in (1, 2, 3)], axis=0
    )
    piece = jnp.concatenate([piece, lax.ppermute(piece, "exp", Z_LO)], axis=0)
    pieces = [piece] + [lax.ppermute(piece, "exp", shift_y(-j)) for j in (1, 2, 3)]

    normed, piece = lax.optimization_barrier((normed, piece))
    partner = lax.ppermute(normed, "exp", Z_LO)
    wq_parts = [wq_part, lax.ppermute(wq_part, "seq", SWAP_X)]
    wq_parts = wq_parts + [lax.ppermute(w, "seq", SIBLING) for w in wq_parts]
    pack = make_pack(pieces, w_expand)
    normed, pack = lax.optimization_barrier((normed, pack))
    q_parts = make_queries(
        jnp.stack([x_at, core, y_at]).astype(jnp.int32), normed, partner, wq_t, wq_parts, cosine, sine
    )
    same_z = [[y * 2 + z for y in range(YS)] for z in range(2)]
    queries = lax.all_to_all(
        q_parts, "exp", split_axis=0, concat_axis=0, axis_index_groups=same_z, tiled=True
    ).reshape(-1, 128)
    plus = lax.ppermute(pack, "seq", shift_x(-1))
    minus = lax.ppermute(pack, "seq", shift_x(1))
    queries, half_a, half_b = lax.optimization_barrier((queries, plus[:UNIT], minus[UNIT:]))
    far_queries = lax.ppermute(queries, "seq", Z_DOWN)
    heads_queries = queries
    far_a = lax.ppermute(half_a, "seq", shift_x(-1))
    far_b = lax.ppermute(half_b, "seq", shift_x(1))
    here = x_at * 2 + core
    stages, modes = [], []
    for held in (((0, pack), (1, plus), (3, minus)), ((2, far_a), (2, far_b))):
        stage, marks = [], []
        for j, mine in held:
            base = ((x_at + j) % XS) * 2
            stage += [mine, lax.ppermute(mine, "seq", SIBLING)]
            marks += [base + core, base + 1 - core]
        stages.append(stage)
        marks = jnp.stack(marks)
        modes.append(jnp.where(marks < here, 1, jnp.where(marks == here, 2, 0)))
    place = jnp.stack([y_at, z_lo, 1 - z_hi])
    carry = None
    for stage, causal in zip(stages, modes):
        marks = jnp.concatenate([jnp.where(z_hi == 0, 1, causal), place]).astype(jnp.int32)
        final = stage is stages[-1]
        carry = attend(marks, (queries, far_queries), stage, carry, last=final, sends=final)
    first, away = carry
    far = lax.ppermute(away, "seq", Z_UP)
    carry = None
    queries, first = lax.optimization_barrier((queries, first))
    for stage, causal in zip(stages, modes):
        marks = jnp.concatenate([jnp.where(z_hi == 0, causal, 0), place]).astype(jnp.int32)
        if carry is not None:
            early = carry[0]
        carry = attend(marks, (queries,), stage, carry, last=stage is stages[-1])
    second, = carry
    attended = finish(jnp.stack([z_hi, z_lo]).astype(jnp.int32), first, far, second)
    by_head = lax.all_to_all(
        attended.reshape(groups, rows, VDIM), "exp", split_axis=0, concat_axis=0, tiled=True
    )

    half_o = w_output.shape[1] // 2
    wo_half = lax.dynamic_slice_in_dim(w_output, core * half_o, half_o, 1)
    wo_half, partner = lax.optimization_barrier((wo_half, partner))
    wo_half = jnp.concatenate([wo_half, lax.ppermute(wo_half, "exp", Z_LO)], axis=0)
    wo_half, heads_queries = lax.optimization_barrier((wo_half, heads_queries))
    shares = [wo_half] + [lax.ppermute(wo_half, "exp", shift_y(-j)) for j in (1, 2, 3)]
    *shares, second = lax.optimization_barrier((*shares, second))
    shares = shares + [lax.ppermute(w, "seq", SIBLING) for w in shares]
    steps = jnp.arange(groups, dtype=jnp.int32)
    near_first = ((y_at + steps // 2) % YS) * 2 + jnp.bitwise_xor(z_lo, steps % 2)

    picked = route_ids[:, :, None] == steps[None, None, :]
    picks = jnp.sum(picked.astype(jnp.int32), axis=1)
    weight = jnp.sum(jnp.where(picked, route_gates[:, :, None], 0.0), axis=1)
    slot = jnp.cumsum(picks, axis=0) - picks
    placed = (slot[:, :, None] == jnp.arange(CAP, dtype=jnp.int32)[None, None, :]) & (
        picks[:, :, None] > 0
    )
    gates = jnp.where(placed, weight[:, :, None], 0.0).reshape(rows, groups * CAP)
    chosen = jnp.transpose(placed.astype(jnp.bfloat16).reshape(rows, groups * CAP))

    mixed, outgoing = middle(
        jnp.concatenate([core[None], near_first]).astype(jnp.int32),
        by_head, shares, tokens, ffn_gain, chosen,
    )
    arrived = lax.all_to_all(outgoing, "exp", split_axis=0, concat_axis=0, tiled=True)
    result = expert(arrived, w_gate_up, w_down)
    returned = lax.all_to_all(result, "exp", split_axis=0, concat_axis=0, tiled=True)
    return combine(mixed, gates, returned)


def solution(mesh):
    placed = (
        P(("seq", "exp"), None),
        P(),
        P(None, "exp"),
        P(),
        P(),
        P(None, "exp"),
        P("exp", None),
        P(),
        P(("seq", "exp"), None),
        P(("seq", "exp"), None),
        P("exp", None, None),
        P("exp", None, None),
    )
    return jax.shard_map(
        body, mesh=mesh, in_specs=placed, out_specs=P(("seq", "exp"), None), check_vma=False
    )
```
